32 devices in a mesh: runs: 2 (over y), row: 4 (over z), col: 2 (over x), sub: 2 (over core).
Axes of the slice: x: 2, y: 2, z: 4, core: 2. Of those that a mesh axis runs over, the one named last changes fastest.
Arguments:
- packed: bfloat16 [4, 2048, 256], P(('col', 'sub'), ('runs', 'row')), parts along dimension 1, may hold values from -6 to 6
- h_real: bfloat16 [8, 4, 128, 128], P('row'), may hold values from -0.25 to 0.25
- h_imag: bfloat16 [8, 4, 128, 128], P('row'), may hold values from -0.25 to 0.25
- h_cols: int32 [8, 4], P('row'), may hold values from 0 to 7, as said below
Outputs:
- evolved: float32 [4, 2048, 256], P(('col', 'sub'), ('runs', 'row')), parts along dimension 1
The draws below stay inside these ranges and needn't reach their ends.
There are 2 independent parts, one for each index of `runs`. The reference program is written for one: setup_inputs(seed, part) draws one part's arguments, and reference() takes and returns one part's arrays. A program takes and returns all parts, laid end to end along the dimension named above; an argument that names none is the same for every part. Nothing has to cross between parts.
Inputs may be any that keep to these rules, and one draw needn't show every extreme that they name: h_cols[b, 0] = b, and h_cols[b, 1], h_cols[b, 2], h_cols[b, 3] are (b + e) mod 8 for three different e among -2, -1, 1, 2.
All inputs are finite; a program needn't handle non-finite values.
Results may differ from the reference program's by a relative error of at most 0.0027.
Values may be sent and summed in bfloat16 or wider, within the bound.
No kernel may reach another device: no remote copies, remote signals or barrier semaphores. Data moves between devices by JAX's collectives and lax.ppermute only.
A program may use at most 64 MiB of HBM per device.

```python
import jax
import jax.numpy as jnp
from jax import lax

BLOCK = 128
TERMS = 3
PIECES = 4
PIECE = 64
BANDS = 4
ORDER = 1024
NBLOCKS = 8


def draw_h_cols(key, part):
    block_rows = jnp.arange(NBLOCKS, dtype=jnp.int32)
    dropped = jax.random.randint(key, (NBLOCKS,), 0, 4).astype(jnp.int32)
    offset_list = jnp.array([-2, -1, 1, 2], dtype=jnp.int32)
    slot_index = jnp.arange(3, dtype=jnp.int32)
    chosen = slot_index[None, :] + (slot_index[None, :] >= dropped[:, None]).astype(jnp.int32)
    kept_offsets = offset_list[chosen]
    offsets = jnp.concatenate([jnp.zeros((NBLOCKS, 1), jnp.int32), kept_offsets], axis=1)
    return ((block_rows[:, None] + offsets) % NBLOCKS).astype(jnp.int32)


def shard_levels(own_key, dims, shards, least, top_value):
    factor_of = 1.0
    for dim, parts in shards:
        draws = jax.random.uniform(jax.random.fold_in(jax.random.fold_in(own_key, 6), dim), (parts,), jnp.float32, least / len(shards), top_value / len(shards))
        factor_of = factor_of * jnp.repeat(jnp.exp(draws), dims[dim] // parts).reshape((-1,) + (1,) * (len(dims) - 1 - dim))
    return factor_of


def bell_draw(stream_key, dims, width, most, shards=(), kind=jnp.bfloat16):
    values = jax.random.normal(stream_key, dims, jnp.float32) * width
    if len(shards) > 0:
        values = shard_levels(stream_key, dims, shards, -0.22, 0.18) * values
    return jnp.clip(values, min=-most, max=most).astype(kind)


def setup_inputs(seed: int = 0, part: int = 0) -> dict:
    key_list = jax.random.split(jax.random.key(seed), 5)
    part_keys = jax.random.split(jax.random.fold_in(key_list[4], part), 5)
    return {
        "packed": bell_draw(part_keys[0], (PIECES, ORDER, BANDS * PIECE), 1.0, 6.0, ((0, 4), (1, 4))),
        "h_real": bell_draw(key_list[1], (NBLOCKS, 4, BLOCK, BLOCK), (4 * BLOCK) ** -0.5, 0.25, ((0, 4),)),
        "h_imag": bell_draw(key_list[2], (NBLOCKS, 4, BLOCK, BLOCK), (4 * BLOCK) ** -0.5, 0.25, ((0, 4),)),
        "h_cols": draw_h_cols(jax.random.fold_in(key_list[4], 71), part),
    }


step_size = 0.5


def unpack(packed):
    grid = packed.reshape(PIECES, ORDER, BANDS, PIECE)
    return jnp.transpose(grid, (1, 2, 0, 3)).reshape(ORDER, ORDER)


def pack_back(matrix):
    grid = matrix.reshape(ORDER, BANDS, PIECES, PIECE)
    return jnp.transpose(grid, (2, 0, 1, 3)).reshape(PIECES, ORDER, BANDS * PIECE)


def reference(packed, h_real, h_imag, h_cols):
    full = unpack(packed)
    mirrored = full.T
    row_ids = jnp.arange(ORDER, dtype=jnp.int32)[:, None]
    col_ids = jnp.arange(ORDER, dtype=jnp.int32)[None, :]
    upper_mask = row_ids <= col_ids
    real_part = jnp.where(upper_mask, full, mirrored)
    imag_part = jnp.where(row_ids > col_ids, full, jnp.where(row_ids < col_ids, -mirrored, jnp.zeros_like(mirrored)))
    current = jnp.stack([real_part, imag_part])
    summed = current.astype(jnp.float32)
    weights = jnp.stack([h_real, h_imag])
    for term_index in range(1, TERMS + 1):
        def one_row(block_row, current=current):
            col_blocks = h_cols[block_row]
            pieces = jax.vmap(lambda column: lax.dynamic_slice_in_dim(current, (column * BLOCK).astype(jnp.int32), BLOCK, 1))(col_blocks)
            row_weights = lax.dynamic_index_in_dim(weights, block_row, 1, keepdims=False)
            product = jnp.einsum("hsij,sgjc->hgic", row_weights.astype(jnp.float32), pieces.astype(jnp.float32))
            real_gen = product[0, 1] + product[1, 0]
            imag_gen = product[1, 1] - product[0, 0]
            return jnp.stack([real_gen, imag_gen]).astype(jnp.bfloat16)

        rows_out = lax.map(one_row, jnp.arange(NBLOCKS, dtype=jnp.int32))
        generator = jnp.transpose(rows_out, (1, 0, 2, 3)).reshape(2, ORDER, ORDER)
        as_float = generator.astype(jnp.float32)
        flipped = jnp.swapaxes(as_float, 1, 2)
        update = (step_size / term_index) * jnp.stack([as_float[0] + flipped[0], as_float[1] - flipped[1]])
        summed = summed + update
        current = update.astype(jnp.bfloat16)
    return pack_back(jnp.where(upper_mask, summed[0], summed[1]))
```

```python
import jax
import jax.numpy as jnp
from jax import lax
from jax.sharding import PartitionSpec as P

TERMS = 3


step_size = 0.5


def extended(block, sides, width):
    for axis, dim in sides:
        count = lax.axis_size(axis)
        forward = [(i, i + 1) for i in range(count - 1)]
        forward.append((count - 1, 0))
        backward = [(target, source) for source, target in forward]
        low = lax.ppermute(
            lax.slice_in_dim(block, block.shape[dim] - width, None, axis=dim), axis, forward
        )
        high = lax.ppermute(lax.slice_in_dim(block, 0, width, axis=dim), axis, backward)
        block = jnp.concatenate([low, block, high], axis=dim)
    return block


def mirror(stacked):
    groups, rows_here, col_count = stacked.shape
    piece_count = lax.axis_size(("col", "sub"))
    band_count = lax.axis_size("row")
    piece_len = rows_here // piece_count
    split_rows = stacked.reshape(groups, piece_count, piece_len, col_count)
    arrived = lax.all_to_all(split_rows, ("col", "sub"), split_axis=1, concat_axis=1, tiled=True)
    turned = jnp.swapaxes(arrived.reshape(groups, rows_here, col_count), 1, 2).reshape(
        groups, band_count, piece_len, rows_here
    )
    landed = lax.all_to_all(turned, "row", split_axis=1, concat_axis=1, tiled=True)
    spread = landed.reshape(groups, band_count, piece_len, piece_count, piece_len)
    placed = jnp.transpose(spread, (0, 3, 2, 1, 4))
    return placed.reshape(groups, rows_here, col_count)


def body(packed, h_real, h_imag, h_cols):
    packed_here = packed.reshape(packed.shape[1], packed.shape[2])
    rows_here, col_count = packed_here.shape
    band_index = lax.axis_index("row")
    piece_index = lax.axis_index(("col", "sub"))
    piece_len = rows_here // lax.axis_size(("col", "sub"))
    flipped = mirror(packed_here[None])[0]
    row_ids = band_index * rows_here + jnp.arange(rows_here, dtype=jnp.int32)[:, None]
    col_local = jnp.arange(col_count, dtype=jnp.int32)[None, :]
    col_ids = col_local // piece_len * rows_here + piece_index * piece_len + col_local % piece_len
    upper_mask = row_ids <= col_ids
    real_part = jnp.where(upper_mask, packed_here, flipped)
    imag_part = jnp.where(
        row_ids > col_ids,
        packed_here,
        jnp.where(row_ids < col_ids, -flipped, jnp.zeros_like(flipped)),
    )
    current = jnp.stack([real_part, imag_part])
    summed = current.astype(jnp.float32)
    combined = jnp.stack([jnp.stack([h_imag, h_real], 2), jnp.stack([-h_real, h_imag], 2)])
    local_blocks = h_real.shape[0]
    block_len = h_real.shape[2]
    block_total = lax.axis_size("row") * local_blocks
    block_ids = band_index * local_blocks + jnp.arange(local_blocks, dtype=jnp.int32)[:, None]
    offsets = (h_cols - block_ids + 2) % block_total - 2
    starts = (
        (jnp.arange(local_blocks, dtype=jnp.int32)[:, None] + offsets + 2) * block_len
    ).reshape(-1)
    for term_index in range(1, TERMS + 1):
        padded = extended(current, (("row", 1),), 2 * block_len)
        sliced = jnp.stack(
            [
                lax.dynamic_slice_in_dim(padded, starts[k], block_len, 1)
                for k in range(starts.shape[0])
            ]
        )
        gathered = sliced.reshape(local_blocks, 4, 2, block_len, col_count)
        product = jnp.einsum(
            "obsgij,bsgjc->obic", combined, gathered, preferred_element_type=jnp.float32
        )
        generator = product.reshape(2, rows_here, col_count).astype(jnp.bfloat16)
        mirror_part = mirror(generator).astype(jnp.float32)
        own_part = generator.astype(jnp.float32)
        update = (
            step_size
            / term_index
            * jnp.stack([own_part[0] + mirror_part[0], own_part[1] - mirror_part[1]])
        )
        summed = summed + update
        current = update.astype(jnp.bfloat16)
    result = jnp.where(upper_mask, summed[0], summed[1])
    return result[None]


def solution(mesh):
    in_specs = (
        P(("col", "sub"), ("runs", "row"), None),
        P("row", None, None, None),
        P("row", None, None, None),
        P("row", None),
    )
    out_specs = P(("col", "sub"), ("runs", "row"), None)
    return jax.shard_map(body, mesh=mesh, in_specs=in_specs, out_specs=out_specs, check_vma=False)
```

```python
import functools

import jax
import jax.numpy as jnp
from jax import lax
from jax.experimental import pallas as pl
from jax.experimental.pallas import tpu as pltpu
from jax.sharding import PartitionSpec as P

TERMS = 3


step_size = 0.5


def extended(block, sides, width):
    for axis, dim in sides:
        count = lax.axis_size(axis)
        forward = [(i, i + 1) for i in range(count - 1)]
        forward.append((count - 1, 0))
        backward = [(target, source) for source, target in forward]
        low = lax.ppermute(
            lax.slice_in_dim(block, block.shape[dim] - width, None, axis=dim), axis, forward
        )
        high = lax.ppermute(lax.slice_in_dim(block, 0, width, axis=dim), axis, backward)
        block = jnp.concatenate([low, block, high], axis=dim)
    return block


def mirror(stacked):
    groups, rows_here, col_count = stacked.shape
    piece_count = lax.axis_size(("col", "sub"))
    band_count = lax.axis_size("row")
    piece_len = rows_here // piece_count
    split_rows = stacked.reshape(groups, piece_count, piece_len, col_count)
    arrived = lax.all_to_all(split_rows, ("col", "sub"), split_axis=1, concat_axis=1, tiled=True)
    turned = jnp.swapaxes(arrived.reshape(groups, rows_here, col_count), 1, 2).reshape(
        groups, band_count, piece_len, rows_here
    )
    landed = lax.all_to_all(turned, "row", split_axis=1, concat_axis=1, tiled=True)
    spread = landed.reshape(groups, band_count, piece_len, piece_count, piece_len)
    placed = jnp.transpose(spread, (0, 3, 2, 1, 4))
    return placed.reshape(groups, rows_here, col_count)


def banded_body(packed, h_real, h_imag, h_cols):
    packed_here = packed.reshape(packed.shape[1], packed.shape[2])
    rows_here, col_count = packed_here.shape
    band_index = lax.axis_index("row")
    piece_index = lax.axis_index(("col", "sub"))
    piece_len = rows_here // lax.axis_size(("col", "sub"))
    flipped = mirror(packed_here[None])[0]
    row_ids = band_index * rows_here + jnp.arange(rows_here, dtype=jnp.int32)[:, None]
    col_local = jnp.arange(col_count, dtype=jnp.int32)[None, :]
    col_ids = col_local // piece_len * rows_here + piece_index * piece_len + col_local % piece_len
    upper_mask = row_ids <= col_ids
    real_part = jnp.where(upper_mask, packed_here, flipped)
    imag_part = jnp.where(
        row_ids > col_ids,
        packed_here,
        jnp.where(row_ids < col_ids, -flipped, jnp.zeros_like(flipped)),
    )
    current = jnp.stack([real_part, imag_part])
    summed = current.astype(jnp.float32)
    combined = jnp.stack([jnp.stack([h_imag, h_real], 2), jnp.stack([-h_real, h_imag], 2)])
    local_blocks = h_real.shape[0]
    block_len = h_real.shape[2]
    block_total = lax.axis_size("row") * local_blocks
    block_ids = band_index * local_blocks + jnp.arange(local_blocks, dtype=jnp.int32)[:, None]
    offsets = (h_cols - block_ids + 2) % block_total - 2
    starts = (
        (jnp.arange(local_blocks, dtype=jnp.int32)[:, None] + offsets + 2) * block_len
    ).reshape(-1)
    for term_index in range(1, TERMS + 1):
        padded = extended(current, (("row", 1),), 2 * block_len)
        sliced = jnp.stack(
            [
                lax.dynamic_slice_in_dim(padded, starts[k], block_len, 1)
                for k in range(starts.shape[0])
            ]
        )
        gathered = sliced.reshape(local_blocks, 4, 2, block_len, col_count)
        product = jnp.einsum(
            "obsgij,bsgjc->obic", combined, gathered, preferred_element_type=jnp.float32
        )
        generator = product.reshape(2, rows_here, col_count).astype(jnp.bfloat16)
        mirror_part = mirror(generator).astype(jnp.float32)
        own_part = generator.astype(jnp.float32)
        update = (
            step_size
            / term_index
            * jnp.stack([own_part[0] + mirror_part[0], own_part[1] - mirror_part[1]])
        )
        summed = summed + update
        current = update.astype(jnp.bfloat16)
    result = jnp.where(upper_mask, summed[0], summed[1])
    return result[None]


VMEM_BYTES = 56 * 2**20
F32 = jnp.float32
BF16 = jnp.bfloat16


def exchange(block, axes, offset):
    count = lax.axis_size(axes)
    return lax.ppermute(block, axes, [(i, i ^ offset) for i in range(count)])


def apply_a(a_ref, v_ref, k, bands, rows, skip):
    order = bands * rows
    slots = [m for m in range(bands) if not (skip and m == k ^ 2)]
    row = slice(k * rows, (k + 1) * rows)
    left = jnp.concatenate(
        [a_ref[row, part * order + m * rows : part * order + (m + 1) * rows] for part in (0, 1) for m in slots],
        axis=1,
    )
    right = jnp.concatenate(
        [v_ref[part * order + m * rows : part * order + (m + 1) * rows, :] for part in (0, 1) for m in slots],
        axis=0,
    )
    return jnp.dot(left, right, preferred_element_type=F32)


def put_v(v_ref, k, value, bands, rows, cols):
    order = bands * rows
    low = value.astype(BF16)
    v_ref[k * rows : (k + 1) * rows, :] = low
    v_ref[order + k * rows : order + (k + 1) * rows, :] = jnp.concatenate(
        [-low[:, cols:], low[:, :cols]], axis=1
    )


def powers_kernel(dims, ids, cols_ref, hr_ref, hi_ref, hg_ref, a_ref, d_ref, va, vb, csum):
    bands, rows, cols, piece, local, count, block, per, skip = dims
    order = bands * rows
    r, q, me_plane, me_core = ids[0], ids[1], ids[2], ids[3]
    a_ref[...] = jnp.zeros_like(a_ref)
    for k in range(bands):
        for b in range(local):
            top = k * rows + b * block
            for s in range(count):
                column = cols_ref[k, b * count + s]
                slot = lax.bitwise_xor(column // local, r)
                place = pl.multiple_of((slot * local + column % local) * block, block)
                for part in (0, 1):
                    if k == 0:
                        got = (hr_ref if part == 0 else hi_ref)[b, s]
                    else:
                        flat = (part * local + b) * count + s
                        share, at = flat // per, flat % per
                        got = hg_ref[
                            lax.bitwise_xor(share % 2, me_core),
                            lax.bitwise_xor(share // 2, me_plane),
                            k - 1,
                            at,
                        ]
                    if part == 0:
                        a_ref[top : top + block, pl.ds(pl.multiple_of(place + order, block), block)] = got * -0.5
                    else:
                        a_ref[top : top + block, pl.ds(place, block)] = got * 0.5
    row_iota = lax.broadcasted_iota(jnp.int32, (rows, cols), 0)
    col_iota = lax.broadcasted_iota(jnp.int32, (rows, cols), 1)
    for k in range(bands):
        hit = (col_iota // piece == lax.bitwise_xor(r, k)) & (row_iota == q * piece + col_iota % piece)
        sel = jnp.where(hit, 1.0, 0.0)
        put_v(va, k, jnp.concatenate([sel, jnp.zeros_like(sel)], axis=1), bands, rows, cols)
    wide = 2 * cols
    for k in range(bands):
        c1 = apply_a(a_ref, va, k, bands, rows, skip)
        put_v(vb, k, c1, bands, rows, cols)
        csum[k * rows : (k + 1) * rows, :] = c1
        d_ref[k * rows : (k + 1) * rows, 2 * wide : 3 * wide] = (0.5 * c1).astype(BF16)
    for k in range(bands):
        c2 = apply_a(a_ref, vb, k, bands, rows, skip)
        put_v(va, k, c2, bands, rows, cols)
        both = csum[k * rows : (k + 1) * rows, :] + 0.5 * c2
        csum[k * rows : (k + 1) * rows, :] = both
        d_ref[k * rows : (k + 1) * rows, wide : 2 * wide] = both.astype(BF16)
    for k in range(bands):
        c3 = apply_a(a_ref, va, k, bands, rows, skip)
        both = csum[k * rows : (k + 1) * rows, :] + c3 * (1.0 / 6.0)
        d_ref[k * rows : (k + 1) * rows, 0:wide] = both.astype(BF16)


def main_kernel(dims, ids, f0_ref, fg_ref, a_ref, d_ref, own_ref, keep_ref, send_ref, va, vb, vsum, right, left, outs):
    bands, rows, cols, piece, local, count, block, per, skip = dims
    pieces = rows // piece
    r, q = ids[0], ids[1]
    wide = 2 * cols
    row_iota = lax.broadcasted_iota(jnp.int32, (rows, cols), 0)
    col_iota = lax.broadcasted_iota(jnp.int32, (rows, cols), 1)
    col_abs = col_iota // piece * rows + q * piece + col_iota % piece
    depth = 4 * cols
    t_re, t_im = 2 * depth, 3 * depth

    def put_t(k, at, value):
        low = value.astype(BF16)
        right[k * rows : (k + 1) * rows, t_re + at * cols : t_re + (at + 1) * cols] = low[:, :cols]
        right[k * rows : (k + 1) * rows, t_im + at * cols : t_im + (at + 1) * cols] = low[:, cols:]

    for k in range(bands):
        here = (f0_ref[...] if k == 0 else fg_ref[k - 1]).astype(F32)
        row_abs = lax.bitwise_xor(r, k) * rows + row_iota
        real = jnp.where(row_abs < col_abs, here, jnp.where(row_abs == col_abs, 0.5 * here, 0.0))
        imag = jnp.where(row_abs > col_abs, here, 0.0)
        value = jnp.concatenate([real, imag], axis=1)
        put_v(va, k, value, bands, rows, cols)
        put_t(k, 1, value)
        hit = (col_iota // piece == lax.bitwise_xor(r, k)) & (row_iota == q * piece + col_iota % piece)
        span = slice(k * rows, (k + 1) * rows)
        right[span, 0:cols] = jnp.where(hit, 1.0, 0.0).astype(BF16)
        right[span, depth : depth + cols] = jnp.zeros((rows, cols), BF16)
        for m in range(3):
            right[span, (m + 1) * cols : (m + 2) * cols] = d_ref[span, m * wide : m * wide + cols]
            right[span, depth + (m + 1) * cols : depth + (m + 2) * cols] = d_ref[span, m * wide + cols : (m + 1) * wide]
    for k in range(bands):
        v1 = apply_a(a_ref, va, k, bands, rows, skip)
        put_v(vb, k, v1, bands, rows, cols)
        put_t(k, 2, v1)
        vsum[k * rows : (k + 1) * rows, :] = v1
    for k in range(bands):
        v2 = apply_a(a_ref, vb, k, bands, rows, skip)
        put_v(va, k, v2, bands, rows, cols)
        put_t(k, 3, v2)
        vsum[k * rows : (k + 1) * rows, :] += 0.5 * v2
    for k in range(bands):
        v3 = apply_a(a_ref, va, k, bands, rows, skip)
        put_t(k, 0, vsum[k * rows : (k + 1) * rows, :] + v3 * (1.0 / 6.0))
    own = slice(0, rows)
    cr, ci = right[own, 0:depth], right[own, depth : 2 * depth]
    tr, ti = right[own, 2 * depth : 3 * depth], right[own, 3 * depth : 4 * depth]
    for n, value in enumerate((tr, ti, cr, ci)):
        left[0, :, n * depth : (n + 1) * depth] = value
    for n, value in enumerate((ti, -tr, ci, -cr)):
        left[1, :, n * depth : (n + 1) * depth] = value
    nt = (((1,), (1,)), ((), ()))

    def against(which, k):
        return lax.dot_general(left[which], right[k * rows : (k + 1) * rows, :], nt, preferred_element_type=F32)

    outs[0] = jnp.where(row_iota <= col_iota[:, :rows], against(0, 0), against(1, 0))
    for k in range(1, bands):
        lower = (lax.bitwise_xor(r, k) < r).astype(jnp.int32)
        outs[k] = against(lower, k)

    def target(piece_index):
        return jnp.concatenate(
            [outs[lax.bitwise_xor(r, b)][:, piece_index * piece : (piece_index + 1) * piece] for b in range(bands)],
            axis=1,
        )

    for p in range(pieces):
        offset = lax.bitwise_xor(q, p)
        value = target(p)

        @pl.when(offset == 0)
        def _():
            own_ref[...] = value

        @pl.when(offset == 2)
        def _():
            keep_ref[...] = value

        @pl.when(offset % 2 == 1)
        def _():
            send_ref[offset // 2] = value.astype(BF16)


def gathered_body(packed, h_real, h_imag, h_cols):
    here = packed.reshape(packed.shape[1], packed.shape[2])
    rows, cols = here.shape
    bands = lax.axis_size("row")
    piece = rows // lax.axis_size(("col", "sub"))
    local, count, block = h_real.shape[0], h_real.shape[1], h_real.shape[2]
    order = bands * rows
    r = lax.axis_index("row")
    q = lax.axis_index(("col", "sub"))
    me_plane = lax.axis_index(("runs", "col"))
    me_core = lax.axis_index("sub")
    shares = lax.axis_size(("runs", "col", "sub"))
    per = 2 * local * count // shares
    skip = bands == 4 and local == 2
    dims = (bands, rows, cols, piece, local, count, block, per, skip)
    ids = jnp.stack([r, q, me_plane, me_core]).astype(jnp.int32)

    all_h = jnp.stack([h_real, h_imag]).reshape(shares, per * block, block)
    share = lax.dynamic_index_in_dim(all_h, me_plane * 2 + me_core, 0, keepdims=False)
    col_row = jnp.pad(h_cols.reshape(1, -1).astype(BF16), ((0, 15), (0, block - local * count)))
    message = jnp.concatenate([share, col_row], axis=0)
    arrived = jnp.stack([exchange(message, "row", k) for k in range(1, bands)])
    their_cols = arrived[:, per * block, : local * count].astype(jnp.int32)
    all_cols = jnp.concatenate([h_cols.reshape(1, -1), their_cols], axis=0)
    mine = arrived[:, : per * block, :]
    plane = jnp.stack([mine] + [exchange(mine, ("runs", "col"), k) for k in range(1, shares // 2)])
    both = jnp.stack([plane, exchange(plane, "sub", 1)])
    both = both.reshape(2, shares // 2, bands - 1, per, block, block)
    rest = jnp.stack([exchange(here, "row", k) for k in range(1, bands)])

    smem = pl.BlockSpec(memory_space=pltpu.SMEM)
    vmem = pl.BlockSpec(memory_space=pltpu.VMEM)
    params = pltpu.CompilerParams(vmem_limit_bytes=VMEM_BYTES)
    step = 2 * order * 2 * order * 2 * cols
    a_big, d_all = pl.pallas_call(
        functools.partial(powers_kernel, dims),
        out_shape=(
            jax.ShapeDtypeStruct((order, 2 * order), BF16),
            jax.ShapeDtypeStruct((order, 6 * cols), BF16),
        ),
        in_specs=[smem, smem, vmem, vmem, vmem],
        out_specs=(vmem, vmem),
        scratch_shapes=[
            pltpu.VMEM((2 * order, 2 * cols), BF16),
            pltpu.VMEM((2 * order, 2 * cols), BF16),
            pltpu.VMEM((order, 2 * cols), F32),
        ],
        compiler_params=params,
        cost_estimate=pl.CostEstimate(flops=3 * step, bytes_accessed=10 * 2**20, transcendentals=0),
        name="powers",
    )(ids, all_cols, h_real, h_imag, both)
    own, keep, send = pl.pallas_call(
        functools.partial(main_kernel, dims),
        out_shape=(
            jax.ShapeDtypeStruct((rows, cols), F32),
            jax.ShapeDtypeStruct((rows, cols), F32),
            jax.ShapeDtypeStruct((2, rows, cols), BF16),
        ),
        in_specs=[smem, vmem, vmem, vmem, vmem],
        out_specs=(vmem, vmem, vmem),
        scratch_shapes=[
            pltpu.VMEM((2 * order, 2 * cols), BF16),
            pltpu.VMEM((2 * order, 2 * cols), BF16),
            pltpu.VMEM((order, 2 * cols), F32),
            pltpu.VMEM((order, 16 * cols), BF16),
            pltpu.VMEM((2, rows, 16 * cols), BF16),
            pltpu.VMEM((bands, rows, rows), F32),
        ],
        compiler_params=params,
        cost_estimate=pl.CostEstimate(flops=6 * step, bytes_accessed=10 * 2**20, transcendentals=0),
        name="main",
    )(ids, here, rest, a_big, d_all)
    swapped = exchange(send, "sub", 1)
    across = exchange((keep + swapped[1].astype(F32)).astype(BF16), "col", 1)
    total = here.astype(F32) + own + swapped[0].astype(F32) + across.astype(F32)
    return total[None]


def can_gather(mesh, local_packed, local_h):
    bands = mesh.shape["row"]
    rows, cols = local_packed[1], local_packed[2]
    local, count, block = local_h[0], local_h[1], local_h[2]
    shares = mesh.shape["runs"] * mesh.shape["col"] * mesh.shape["sub"]
    return (
        bands & (bands - 1) == 0
        and mesh.shape["runs"] == mesh.shape["col"] == mesh.shape["sub"] == 2
        and rows == cols == local * block
        and (2 * local * count) % shares == 0
        and local * count <= block
        and 80 * bands * rows * bands * rows // 2 <= VMEM_BYTES
    )


def body(mesh, packed, h_real, h_imag, h_cols):
    if can_gather(mesh, packed.shape, h_real.shape):
        return gathered_body(packed, h_real, h_imag, h_cols)
    return banded_body(packed, h_real, h_imag, h_cols)


def solution(mesh):
    in_specs = (
        P(("col", "sub"), ("runs", "row"), None),
        P("row", None, None, None),
        P("row", None, None, None),
        P("row", None),
    )
    out_specs = P(("col", "sub"), ("runs", "row"), None)
    return jax.shard_map(
        functools.partial(body, mesh), mesh=mesh, in_specs=in_specs, out_specs=out_specs, check_vma=False
    )
```

```python
import functools

import jax
import jax.numpy as jnp
from jax import lax
from jax.experimental import pallas as pl
from jax.experimental.pallas import tpu as pltpu
from jax.sharding import PartitionSpec as P

TERMS = 3


step_size = 0.5


def extended(block, sides, width):
    for axis, dim in sides:
        count = lax.axis_size(axis)
        forward = [(i, i + 1) for i in range(count - 1)]
        forward.append((count - 1, 0))
        backward = [(target, source) for source, target in forward]
        low = lax.ppermute(
            lax.slice_in_dim(block, block.shape[dim] - width, None, axis=dim), axis, forward
        )
        high = lax.ppermute(lax.slice_in_dim(block, 0, width, axis=dim), axis, backward)
        block = jnp.concatenate([low, block, high], axis=dim)
    return block


def mirror(stacked):
    groups, rows_here, col_count = stacked.shape
    piece_count = lax.axis_size(("col", "sub"))
    band_count = lax.axis_size("row")
    piece_len = rows_here // piece_count
    split_rows = stacked.reshape(groups, piece_count, piece_len, col_count)
    arrived = lax.all_to_all(split_rows, ("col", "sub"), split_axis=1, concat_axis=1, tiled=True)
    turned = jnp.swapaxes(arrived.reshape(groups, rows_here, col_count), 1, 2).reshape(
        groups, band_count, piece_len, rows_here
    )
    landed = lax.all_to_all(turned, "row", split_axis=1, concat_axis=1, tiled=True)
    spread = landed.reshape(groups, band_count, piece_len, piece_count, piece_len)
    placed = jnp.transpose(spread, (0, 3, 2, 1, 4))
    return placed.reshape(groups, rows_here, col_count)


def banded_body(packed, h_real, h_imag, h_cols):
    packed_here = packed.reshape(packed.shape[1], packed.shape[2])
    rows_here, col_count = packed_here.shape
    band_index = lax.axis_index("row")
    piece_index = lax.axis_index(("col", "sub"))
    piece_len = rows_here // lax.axis_size(("col", "sub"))
    flipped = mirror(packed_here[None])[0]
    row_ids = band_index * rows_here + jnp.arange(rows_here, dtype=jnp.int32)[:, None]
    col_local = jnp.arange(col_count, dtype=jnp.int32)[None, :]
    col_ids = col_local // piece_len * rows_here + piece_index * piece_len + col_local % piece_len
    upper_mask = row_ids <= col_ids
    real_part = jnp.where(upper_mask, packed_here, flipped)
    imag_part = jnp.where(
        row_ids > col_ids,
        packed_here,
        jnp.where(row_ids < col_ids, -flipped, jnp.zeros_like(flipped)),
    )
    current = jnp.stack([real_part, imag_part])
    summed = current.astype(jnp.float32)
    combined = jnp.stack([jnp.stack([h_imag, h_real], 2), jnp.stack([-h_real, h_imag], 2)])
    local_blocks = h_real.shape[0]
    block_len = h_real.shape[2]
    block_total = lax.axis_size("row") * local_blocks
    block_ids = band_index * local_blocks + jnp.arange(local_blocks, dtype=jnp.int32)[:, None]
    offsets = (h_cols - block_ids + 2) % block_total - 2
    starts = (
        (jnp.arange(local_blocks, dtype=jnp.int32)[:, None] + offsets + 2) * block_len
    ).reshape(-1)
    for term_index in range(1, TERMS + 1):
        padded = extended(current, (("row", 1),), 2 * block_len)
        sliced = jnp.stack(
            [
                lax.dynamic_slice_in_dim(padded, starts[k], block_len, 1)
                for k in range(starts.shape[0])
            ]
        )
        gathered = sliced.reshape(local_blocks, 4, 2, block_len, col_count)
        product = jnp.einsum(
            "obsgij,bsgjc->obic", combined, gathered, preferred_element_type=jnp.float32
        )
        generator = product.reshape(2, rows_here, col_count).astype(jnp.bfloat16)
        mirror_part = mirror(generator).astype(jnp.float32)
        own_part = generator.astype(jnp.float32)
        update = (
            step_size
            / term_index
            * jnp.stack([own_part[0] + mirror_part[0], own_part[1] - mirror_part[1]])
        )
        summed = summed + update
        current = update.astype(jnp.bfloat16)
    result = jnp.where(upper_mask, summed[0], summed[1])
    return result[None]


VMEM_BYTES = 56 * 2**20
POWERS_VMEM = 22 * 2**20
MAIN_VMEM = 30 * 2**20
F32 = jnp.float32
BF16 = jnp.bfloat16


def exchange(block, axes, offset):
    count = lax.axis_size(axes)
    return lax.ppermute(block, axes, [(i, i ^ offset) for i in range(count)])


def apply_a(a_ref, v_ref, k, bands, rows, skip):
    order = bands * rows
    slots = [m for m in range(bands) if not (skip and m == k ^ 2)]
    row = slice(k * rows, (k + 1) * rows)
    left = jnp.concatenate(
        [a_ref[row, part * order + m * rows : part * order + (m + 1) * rows] for part in (0, 1) for m in slots],
        axis=1,
    )
    right = jnp.concatenate(
        [v_ref[part * order + m * rows : part * order + (m + 1) * rows, :] for part in (0, 1) for m in slots],
        axis=0,
    )
    return jnp.dot(left, right, preferred_element_type=F32)


def put_v(v_ref, k, value, bands, rows, cols):
    order = bands * rows
    low = value.astype(BF16)
    v_ref[k * rows : (k + 1) * rows, :] = low
    v_ref[order + k * rows : order + (k + 1) * rows, :] = jnp.concatenate(
        [-low[:, cols:], low[:, :cols]], axis=1
    )


def place_blocks(dims, r, me_plane, facts, slots, find, a_ref):
    bands, rows, cols, piece, local, count, block, per, skip = dims
    order = bands * rows
    for k in slots:
        for b in range(local):
            top = k * rows + b * block
            for s in range(count):
                column = facts[4 + k * local * count + b * count + s]
                slot = lax.bitwise_xor(column // local, r)
                place = pl.multiple_of((slot * local + column % local) * block, block)
                imag = pl.multiple_of(place + order, block)
                a_ref[top : top + block, pl.ds(place, block)] = find(k, 1, b, s) * 0.5
                a_ref[top : top + block, pl.ds(imag, block)] = find(k, 0, b, s) * -0.5


def powers_kernel(dims, facts, hr_ref, hi_ref, near_ref, far_ref, a_ref, c_ref, va, vb, csum):
    bands, rows, cols, piece, local, count, block, per, skip = dims
    r, q, me_plane, me_core = facts[0], facts[1], facts[2], facts[3]
    a_ref[...] = jnp.zeros_like(a_ref)
    place_blocks(
        dims, r, me_plane, facts, [0], lambda k, part, b, s: (hi_ref if part else hr_ref)[b, s], a_ref
    )

    def from_core(refs):
        def find(k, part, b, s):
            flat = (part * local + b) * count + s
            share, at = flat // per, flat % per
            return refs[share % 2][lax.bitwise_xor(share // 2, me_plane), k - 1, at]

        place_blocks(dims, r, me_plane, facts, list(range(1, bands)), find, a_ref)

    @pl.when(me_core == 0)
    def _():
        from_core((near_ref, far_ref))

    @pl.when(me_core == 1)
    def _():
        from_core((far_ref, near_ref))

    row_iota = lax.broadcasted_iota(jnp.int32, (rows, cols), 0)
    col_iota = lax.broadcasted_iota(jnp.int32, (rows, cols), 1)
    for k in range(bands):
        hit = (col_iota // piece == lax.bitwise_xor(r, k)) & (row_iota == q * piece + col_iota % piece)
        c_ref[k * rows : (k + 1) * rows, 0:cols] = jnp.where(hit, 1.0, 0.0).astype(BF16)

    def put_d(k, m, value):
        low = value.astype(BF16)
        c_ref[k * rows : (k + 1) * rows, m * cols : (m + 1) * cols] = low[:, :cols]
        c_ref[k * rows : (k + 1) * rows, (m + 3) * cols : (m + 4) * cols] = low[:, cols:]

    order = bands * rows
    for k in range(bands):
        slots = [m for m in range(bands) if not (skip and m == k ^ 2)]
        row = slice(k * rows, (k + 1) * rows)
        sel = jnp.concatenate([c_ref[m * rows : (m + 1) * rows, 0:cols] for m in slots], axis=0)
        both = [
            jnp.dot(
                jnp.concatenate(
                    [a_ref[row, part * order + m * rows : part * order + (m + 1) * rows] for m in slots], axis=1
                ),
                sel,
                preferred_element_type=F32,
            )
            for part in (0, 1)
        ]
        c1 = jnp.concatenate(both, axis=1)
        put_v(vb, k, c1, bands, rows, cols)
        csum[row, :] = c1
        put_d(k, 3, 0.5 * c1)
    for k in range(bands):
        c2 = apply_a(a_ref, vb, k, bands, rows, skip)
        put_v(va, k, c2, bands, rows, cols)
        both = csum[k * rows : (k + 1) * rows, :] + 0.5 * c2
        csum[k * rows : (k + 1) * rows, :] = both
        put_d(k, 2, both)
    for k in range(bands):
        c3 = apply_a(a_ref, va, k, bands, rows, skip)
        put_d(k, 1, csum[k * rows : (k + 1) * rows, :] + c3 * (1.0 / 6.0))


def main_kernel(dims, facts, *refs):
    bands, rows, cols, piece, local, count, block, per, skip = dims
    f_refs = refs[:bands]
    a_ref, c_ref, own_ref, keep_ref, send_ref, va, vb, vsum, t_ref, left, outs = refs[bands:]
    pieces = rows // piece
    r, q = facts[0], facts[1]
    row_iota = lax.broadcasted_iota(jnp.int32, (rows, cols), 0)
    col_iota = lax.broadcasted_iota(jnp.int32, (rows, cols), 1)
    col_abs = col_iota // piece * rows + q * piece + col_iota % piece

    def put_t(k, at, value):
        low = value.astype(BF16)
        t_ref[k * rows : (k + 1) * rows, at * cols : (at + 1) * cols] = low[:, :cols]
        t_ref[k * rows : (k + 1) * rows, (at + 4) * cols : (at + 5) * cols] = low[:, cols:]

    for k in range(bands):
        here = f_refs[k][...].astype(F32)
        row_abs = lax.bitwise_xor(r, k) * rows + row_iota
        real = jnp.where(row_abs < col_abs, here, jnp.where(row_abs == col_abs, 0.5 * here, 0.0))
        imag = jnp.where(row_abs > col_abs, here, 0.0)
        value = jnp.concatenate([real, imag], axis=1)
        put_v(va, k, value, bands, rows, cols)
        put_t(k, 1, value)
    for k in range(bands):
        v1 = apply_a(a_ref, va, k, bands, rows, skip)
        put_v(vb, k, v1, bands, rows, cols)
        put_t(k, 2, v1)
        vsum[k * rows : (k + 1) * rows, :] = v1
    for k in range(bands):
        v2 = apply_a(a_ref, vb, k, bands, rows, skip)
        put_v(va, k, v2, bands, rows, cols)
        put_t(k, 3, v2)
        vsum[k * rows : (k + 1) * rows, :] += 0.5 * v2
    for k in range(bands):
        v3 = apply_a(a_ref, va, k, bands, rows, skip)
        put_t(k, 0, vsum[k * rows : (k + 1) * rows, :] + v3 * (1.0 / 6.0))
    own = slice(0, rows)
    half = 7 * cols
    for which, values in enumerate(
        (
            (t_ref[own, 0 : 4 * cols], t_ref[own, 5 * cols : 8 * cols]),
            (t_ref[own, 4 * cols : 8 * cols], -t_ref[own, cols : 4 * cols]),
        )
    ):
        left[which, :, 0 : 4 * cols] = values[0]
        left[which, :, 4 * cols : half] = values[1]
    cr, ci = c_ref[own, 0 : 4 * cols], c_ref[own, 4 * cols : half]
    none = jnp.zeros((rows, cols), BF16)
    left[0, :, half : half + 4 * cols] = cr
    left[0, :, half + 4 * cols : half + 5 * cols] = none
    left[0, :, half + 5 * cols : half + 8 * cols] = ci
    left[1, :, half : half + cols] = none
    left[1, :, half + cols : half + 4 * cols] = ci
    left[1, :, half + 4 * cols : half + 8 * cols] = -cr
    nt = (((1,), (1,)), ((), ()))

    def against(which, k):
        right = jnp.concatenate(
            [c_ref[k * rows : (k + 1) * rows, :], t_ref[k * rows : (k + 1) * rows, :]], axis=1
        )
        return lax.dot_general(left[which], right, nt, preferred_element_type=F32)

    outs[0] = jnp.where(row_iota <= col_iota[:, :rows], against(0, 0), against(1, 0))
    for k in range(1, bands):
        lower = (lax.bitwise_xor(r, k) < r).astype(jnp.int32)
        outs[k] = against(lower, k)

    def target(piece_index):
        return jnp.concatenate(
            [outs[lax.bitwise_xor(r, b)][:, piece_index * piece : (piece_index + 1) * piece] for b in range(bands)],
            axis=1,
        )

    for p in range(pieces):
        offset = lax.bitwise_xor(q, p)
        value = target(p)

        @pl.when(offset == 0)
        def _():
            own_ref[...] = value

        @pl.when(offset == 2)
        def _():
            keep_ref[...] = value

        @pl.when(offset % 2 == 1)
        def _():
            send_ref[offset // 2] = value.astype(BF16)


def gathered_body(packed, h_real, h_imag, h_cols):
    here = packed.reshape(packed.shape[1], packed.shape[2])
    rows, cols = here.shape
    bands = lax.axis_size("row")
    piece = rows // lax.axis_size(("col", "sub"))
    local, count, block = h_real.shape[0], h_real.shape[1], h_real.shape[2]
    order = bands * rows
    r = lax.axis_index("row")
    q = lax.axis_index(("col", "sub"))
    me_plane = lax.axis_index(("runs", "col"))
    me_core = lax.axis_index("sub")
    shares = lax.axis_size(("runs", "col", "sub"))
    per = 2 * local * count // shares
    skip = bands == 4 and local == 2
    dims = (bands, rows, cols, piece, local, count, block, per, skip)

    start = q * per
    share = jnp.where(
        lax.axis_index("runs") == 0,
        lax.dynamic_slice_in_dim(h_real.reshape(local * count, block, block), start, per, 0),
        lax.dynamic_slice_in_dim(h_imag.reshape(local * count, block, block), start, per, 0),
    ).reshape(per * block, block)
    col_row = jnp.pad(h_cols.reshape(1, -1).astype(BF16), ((0, 15), (0, block - local * count)))
    message = jnp.concatenate([share, col_row], axis=0)
    arrived = [exchange(message, "row", k) for k in range(1, bands)]
    their_cols = [a[per * block, : local * count].astype(jnp.int32) for a in arrived]
    facts = jnp.concatenate(
        [jnp.stack([r, q, me_plane, me_core]).astype(jnp.int32), h_cols.reshape(-1)] + their_cols
    )
    mine = jnp.stack([a[: per * block] for a in arrived])
    plane = jnp.stack([mine] + [exchange(mine, ("runs", "col"), k) for k in range(1, shares // 2)])
    far = exchange(plane, "sub", 1)
    near, far = [x.reshape(shares // 2, bands - 1, per, block, block) for x in (plane, far)]
    rest = [exchange(here, "row", k) for k in range(1, bands)]

    smem = pl.BlockSpec(memory_space=pltpu.SMEM)
    vmem = pl.BlockSpec(memory_space=pltpu.VMEM)
    step = 2 * order * 2 * order * 2 * cols
    a_big, c_side = pl.pallas_call(
        functools.partial(powers_kernel, dims),
        out_shape=(
            jax.ShapeDtypeStruct((order, 2 * order), BF16),
            jax.ShapeDtypeStruct((order, 7 * cols), BF16),
        ),
        in_specs=[smem] + [vmem] * 4,
        out_specs=(vmem, vmem),
        scratch_shapes=[
            pltpu.VMEM((2 * order, 2 * cols), BF16),
            pltpu.VMEM((2 * order, 2 * cols), BF16),
            pltpu.VMEM((order, 2 * cols), F32),
        ],
        compiler_params=pltpu.CompilerParams(vmem_limit_bytes=POWERS_VMEM),
        cost_estimate=pl.CostEstimate(flops=4 * step, bytes_accessed=10 * 2**20, transcendentals=0),
        name="powers",
    )(facts, h_real, h_imag, near, far)
    own, keep, send = pl.pallas_call(
        functools.partial(main_kernel, dims),
        out_shape=(
            jax.ShapeDtypeStruct((rows, cols), F32),
            jax.ShapeDtypeStruct((rows, cols), F32),
            jax.ShapeDtypeStruct((2, rows, cols), BF16),
        ),
        in_specs=[smem] + [vmem] * (bands + 2),
        out_specs=(vmem, vmem, vmem),
        scratch_shapes=[
            pltpu.VMEM((2 * order, 2 * cols), BF16),
            pltpu.VMEM((2 * order, 2 * cols), BF16),
            pltpu.VMEM((order, 2 * cols), F32),
            pltpu.VMEM((order, 8 * cols), BF16),
            pltpu.VMEM((2, rows, 15 * cols), BF16),
            pltpu.VMEM((bands, rows, rows), F32),
        ],
        compiler_params=pltpu.CompilerParams(vmem_limit_bytes=MAIN_VMEM),
        cost_estimate=pl.CostEstimate(flops=6 * step, bytes_accessed=10 * 2**20, transcendentals=0),
        name="main",
    )(facts, here, *rest, a_big, c_side)
    swapped = exchange(send, "sub", 1)
    across = exchange((keep + swapped[1].astype(F32)).astype(BF16), "col", 1)
    total = here.astype(F32) + own + swapped[0].astype(F32) + across.astype(F32)
    return total[None]


def can_gather(mesh, local_packed, local_h):
    bands = mesh.shape["row"]
    rows, cols = local_packed[1], local_packed[2]
    local, count, block = local_h[0], local_h[1], local_h[2]
    shares = mesh.shape["runs"] * mesh.shape["col"] * mesh.shape["sub"]
    return (
        bands & (bands - 1) == 0
        and mesh.shape["runs"] == mesh.shape["col"] == mesh.shape["sub"] == 2
        and rows == cols == local * block
        and (2 * local * count) % shares == 0
        and local * count <= block
        and 80 * bands * rows * bands * rows // 2 <= VMEM_BYTES
    )


def body(mesh, packed, h_real, h_imag, h_cols):
    if can_gather(mesh, packed.shape, h_real.shape):
        return gathered_body(packed, h_real, h_imag, h_cols)
    return banded_body(packed, h_real, h_imag, h_cols)


def solution(mesh):
    in_specs = (
        P(("col", "sub"), ("runs", "row"), None),
        P("row", None, None, None),
        P("row", None, None, None),
        P("row", None),
    )
    out_specs = P(("col", "sub"), ("runs", "row"), None)
    return jax.shard_map(
        functools.partial(body, mesh), mesh=mesh, in_specs=in_specs, out_specs=out_specs, check_vma=False
    )
```

```python
import functools

import jax
import jax.numpy as jnp
from jax import lax
from jax.experimental import pallas as pl
from jax.experimental.pallas import tpu as pltpu
from jax.sharding import PartitionSpec as P

TERMS = 3


step_size = 0.5


def extended(block, sides, width):
    for axis, dim in sides:
        count = lax.axis_size(axis)
        forward = [(i, i + 1) for i in range(count - 1)]
        forward.append((count - 1, 0))
        backward = [(target, source) for source, target in forward]
        low = lax.ppermute(
            lax.slice_in_dim(block, block.shape[dim] - width, None, axis=dim), axis, forward
        )
        high = lax.ppermute(lax.slice_in_dim(block, 0, width, axis=dim), axis, backward)
        block = jnp.concatenate([low, block, high], axis=dim)
    return block


def mirror(stacked):
    groups, rows_here, col_count = stacked.shape
    piece_count = lax.axis_size(("col", "sub"))
    band_count = lax.axis_size("row")
    piece_len = rows_here // piece_count
    split_rows = stacked.reshape(groups, piece_count, piece_len, col_count)
    arrived = lax.all_to_all(split_rows, ("col", "sub"), split_axis=1, concat_axis=1, tiled=True)
    turned = jnp.swapaxes(arrived.reshape(groups, rows_here, col_count), 1, 2).reshape(
        groups, band_count, piece_len, rows_here
    )
    landed = lax.all_to_all(turned, "row", split_axis=1, concat_axis=1, tiled=True)
    spread = landed.reshape(groups, band_count, piece_len, piece_count, piece_len)
    placed = jnp.transpose(spread, (0, 3, 2, 1, 4))
    return placed.reshape(groups, rows_here, col_count)


def banded_body(packed, h_real, h_imag, h_cols):
    packed_here = packed.reshape(packed.shape[1], packed.shape[2])
    rows_here, col_count = packed_here.shape
    band_index = lax.axis_index("row")
    piece_index = lax.axis_index(("col", "sub"))
    piece_len = rows_here // lax.axis_size(("col", "sub"))
    flipped = mirror(packed_here[None])[0]
    row_ids = band_index * rows_here + jnp.arange(rows_here, dtype=jnp.int32)[:, None]
    col_local = jnp.arange(col_count, dtype=jnp.int32)[None, :]
    col_ids = col_local // piece_len * rows_here + piece_index * piece_len + col_local % piece_len
    upper_mask = row_ids <= col_ids
    real_part = jnp.where(upper_mask, packed_here, flipped)
    imag_part = jnp.where(
        row_ids > col_ids,
        packed_here,
        jnp.where(row_ids < col_ids, -flipped, jnp.zeros_like(flipped)),
    )
    current = jnp.stack([real_part, imag_part])
    summed = current.astype(jnp.float32)
    combined = jnp.stack([jnp.stack([h_imag, h_real], 2), jnp.stack([-h_real, h_imag], 2)])
    local_blocks = h_real.shape[0]
    block_len = h_real.shape[2]
    block_total = lax.axis_size("row") * local_blocks
    block_ids = band_index * local_blocks + jnp.arange(local_blocks, dtype=jnp.int32)[:, None]
    offsets = (h_cols - block_ids + 2) % block_total - 2
    starts = (
        (jnp.arange(local_blocks, dtype=jnp.int32)[:, None] + offsets + 2) * block_len
    ).reshape(-1)
    for term_index in range(1, TERMS + 1):
        padded = extended(current, (("row", 1),), 2 * block_len)
        sliced = jnp.stack(
            [
                lax.dynamic_slice_in_dim(padded, starts[k], block_len, 1)
                for k in range(starts.shape[0])
            ]
        )
        gathered = sliced.reshape(local_blocks, 4, 2, block_len, col_count)
        product = jnp.einsum(
            "obsgij,bsgjc->obic", combined, gathered, preferred_element_type=jnp.float32
        )
        generator = product.reshape(2, rows_here, col_count).astype(jnp.bfloat16)
        mirror_part = mirror(generator).astype(jnp.float32)
        own_part = generator.astype(jnp.float32)
        update = (
            step_size
            / term_index
            * jnp.stack([own_part[0] + mirror_part[0], own_part[1] - mirror_part[1]])
        )
        summed = summed + update
        current = update.astype(jnp.bfloat16)
    result = jnp.where(upper_mask, summed[0], summed[1])
    return result[None]


VMEM_BYTES = 56 * 2**20
POWERS_VMEM = 20 * 2**20
MAIN_VMEM = 24 * 2**20
F32 = jnp.float32
BF16 = jnp.bfloat16


def exchange(block, axes, offset):
    count = lax.axis_size(axes)
    return lax.ppermute(block, axes, [(i, i ^ offset) for i in range(count)])


def block_product(dims, facts, h_ref, at, take):
    bands, rows, cols, piece, local, count, block, per = dims
    starts = []
    for s in range(count):
        column = facts[4 + at * count + s]
        slot = lax.bitwise_xor(column // local, facts[0])
        starts.append(pl.multiple_of((slot * local + column % local) * block, block))
    right = jnp.concatenate([take(pl.ds(start, block)) for start in starts], axis=0)
    return jnp.dot(h_ref[at], right, preferred_element_type=F32)


def apply_a(dims, facts, h_ref, at, take, width):
    block = dims[6]
    got = block_product(dims, facts, h_ref, at, take)
    real = got[:block, :width] + got[block:, width:]
    imag = got[:block, width:] - got[block:, :width]
    return 0.5 * jnp.concatenate([real, imag], axis=1)


def powers_kernel(dims, facts, mine_ref, near_ref, far_ref, h_ref, c_ref, sel, c1_ref, c2_ref, csum):
    bands, rows, cols, piece, local, count, block, per = dims
    r, q, me_plane, me_core = facts[0], facts[1], facts[2], facts[3]
    h_ref[0:local] = mine_ref[...]
    for n in range(2 * near_ref.shape[0]):
        part = (near_ref, far_ref)[n % 2]
        share = lax.bitwise_xor(me_plane, n // 2) * 2 + lax.bitwise_xor(me_core, n % 2)
        for at in range(per):
            flat = share * per + at
            below = pl.multiple_of((1 - flat // (local * count)) * block, block)
            b = flat // count % local
            beside = pl.multiple_of(flat % count * block, block)
            for k in range(1, bands):
                h_ref[k * local + b, pl.ds(below, block), pl.ds(beside, block)] = part[
                    n // 2, k - 1, at * block : (at + 1) * block, :
                ]
    row_iota = lax.broadcasted_iota(jnp.int32, (rows, cols), 0)
    col_iota = lax.broadcasted_iota(jnp.int32, (rows, cols), 1)
    for k in range(bands):
        hit = (col_iota // piece == k) & (row_iota == q * piece + col_iota % piece)
        sel[k * rows : (k + 1) * rows, :] = jnp.where(hit, 1.0, 0.0).astype(BF16)

    def put_d(span, m, value):
        low = value.astype(BF16)
        c_ref[span, m * cols : (m + 1) * cols] = low[:, :cols]
        c_ref[span, (m + 3) * cols : (m + 4) * cols] = low[:, cols:]

    for at in range(bands * local):
        span = slice(at * block, (at + 1) * block)
        got = block_product(dims, facts, h_ref, at, lambda where: sel[where, :])
        c1 = 0.5 * jnp.concatenate([got[:block], -got[block:]], axis=1)
        c1_ref[span, :] = c1.astype(BF16)
        csum[span, :] = c1
        put_d(span, 2, 0.5 * c1)
    for at in range(bands * local):
        span = slice(at * block, (at + 1) * block)
        c2 = apply_a(dims, facts, h_ref, at, lambda where: c1_ref[where, :], cols)
        c2_ref[span, :] = c2.astype(BF16)
        both = csum[span, :] + 0.5 * c2
        csum[span, :] = both
        put_d(span, 1, both)
    for at in range(bands * local):
        span = slice(at * block, (at + 1) * block)
        c3 = apply_a(dims, facts, h_ref, at, lambda where: c2_ref[where, :], cols)
        put_d(span, 0, csum[span, :] + c3 * (1.0 / 6.0))


def swap_groups(value, r, piece):
    size = value.shape[1]
    groups = size // piece
    bit = 1
    while bit < groups:
        moved = jnp.concatenate(
            [value[:, (g ^ bit) * piece : (g ^ bit) * piece + piece] for g in range(groups)], axis=1
        )
        value = jnp.where(lax.bitwise_and(r, bit) != 0, moved, value)
        bit *= 2
    return value


def main_kernel(dims, facts, *refs):
    bands, rows, cols, piece, local, count, block, per = dims
    f_refs = refs[:bands]
    h_ref, c_ref, own_ref, keep_ref, send_ref, n_ref, v1_ref, v2_ref, slab, tops, left, outs = refs[bands:]
    pieces = rows // piece
    r, q = facts[0], facts[1]
    row_iota = lax.broadcasted_iota(jnp.int32, (rows, cols), 0)
    col_iota = lax.broadcasted_iota(jnp.int32, (rows, cols), 1)
    col_abs = col_iota // piece * rows + q * piece + col_iota % piece
    for k in range(bands):
        here = f_refs[k][...].astype(F32)
        row_abs = lax.bitwise_xor(r, k) * rows + row_iota
        real = jnp.where(row_abs < col_abs, here, jnp.where(row_abs == col_abs, 0.5 * here, 0.0))
        imag = jnp.where(row_abs > col_abs, here, 0.0)
        for half, value in enumerate((real, imag)):
            n_ref[k * rows : (k + 1) * rows, half * cols : (half + 1) * cols] = swap_groups(
                value, r, piece
            ).astype(BF16)

    def thin(value):
        return jnp.concatenate([value[:, :piece], value[:, cols : cols + piece]], axis=1)

    for at in range(bands * local):
        span = slice(at * block, (at + 1) * block)
        v1 = apply_a(dims, facts, h_ref, at, lambda where: n_ref[where, :], cols)
        v1_ref[span, :] = v1.astype(BF16)
        slab[span, :] = thin(v1)
        if at < local:
            tops[span, :] = v1
    for at in range(bands * local):
        span = slice(at * block, (at + 1) * block)
        v2 = apply_a(dims, facts, h_ref, at, lambda where: v1_ref[where, :], cols)
        v2_ref[span, :] = v2.astype(BF16)
        slab[span, :] += 0.5 * thin(v2)
        if at < local:
            tops[span, :] += 0.5 * v2
    for at in range(bands * local):
        span = slice(at * block, (at + 1) * block)
        if at < local:
            v3 = apply_a(dims, facts, h_ref, at, lambda where: v2_ref[where, :], cols)
            tops[span, :] += v3 * (1.0 / 6.0)
            slab[span, :] += thin(v3) * (1.0 / 6.0)
        else:
            v3 = apply_a(
                dims,
                facts,
                h_ref,
                at,
                lambda where: jnp.concatenate(
                    [v2_ref[where, 0:piece], v2_ref[where, cols : cols + piece]],
                    axis=1,
                ),
                piece,
            )
            slab[span, :] += v3 * (1.0 / 6.0)
    own = slice(0, rows)
    three = 3 * cols
    for m, t_ref in enumerate((n_ref, v1_ref, v2_ref)):
        tr, ti = t_ref[own, :cols], t_ref[own, cols:]
        cr = c_ref[own, m * cols : (m + 1) * cols]
        ci = c_ref[own, three + m * cols : three + (m + 1) * cols]
        for which, (first, second, third, fourth) in enumerate(((tr, ti, cr, ci), (ti, -tr, ci, -cr))):
            left[which, :, m * cols : (m + 1) * cols] = first
            left[which, :, three + m * cols : three + (m + 1) * cols] = second
            left[which, :, 2 * three + 2 * m * cols : 2 * three + (2 * m + 1) * cols] = third
            left[which, :, 2 * three + (2 * m + 1) * cols : 2 * three + (2 * m + 2) * cols] = fourth
    nt = (((1,), (1,)), ((), ()))

    def against(which, k):
        span = slice(k * rows, (k + 1) * rows)
        right = jnp.concatenate([ref[span, :] for ref in (c_ref, n_ref, v1_ref, v2_ref)], axis=1)
        return lax.dot_general(left[which], right, nt, preferred_element_type=F32)

    upper = row_iota[:, :rows] <= lax.broadcasted_iota(jnp.int32, (rows, rows), 1)
    mine = pl.ds(pl.multiple_of(q * piece, piece), piece)
    thin_row = q * piece + lax.broadcasted_iota(jnp.int32, (piece, rows), 0)
    thin_upper = thin_row <= lax.broadcasted_iota(jnp.int32, (piece, rows), 1)
    outs[0] = jnp.where(upper, against(0, 0), against(1, 0))
    for k in range(1, bands):
        lower = (lax.bitwise_xor(r, k) < r).astype(jnp.int32)
        outs[k] = against(lower, k)
    for k in range(bands):
        turned = slab[k * rows : (k + 1) * rows, :].T
        real, imag = turned[:piece], -turned[piece:]
        if k == 0:
            extra = jnp.where(thin_upper, real, imag)
        else:
            extra = jnp.where(lax.bitwise_xor(r, k) > r, real, imag)
        outs[k, mine, :] += extra

    def target(piece_index):
        return jnp.concatenate(
            [outs[lax.bitwise_xor(r, b)][:, piece_index * piece : (piece_index + 1) * piece] for b in range(bands)],
            axis=1,
        )

    for p in range(pieces):
        offset = lax.bitwise_xor(q, p)
        value = target(p)

        @pl.when(offset == 0)
        def _():
            real = swap_groups(tops[:, :cols], r, piece)
            imag = swap_groups(tops[:, cols:], r, piece)
            own_ref[...] = value + jnp.where(r * rows + row_iota <= col_abs, real, imag)

        @pl.when(offset == 2)
        def _():
            keep_ref[...] = value

        @pl.when(offset % 2 == 1)
        def _():
            send_ref[offset // 2] = value.astype(BF16)


def gathered_body(packed, h_real, h_imag, h_cols):
    here = packed.reshape(packed.shape[1], packed.shape[2])
    rows, cols = here.shape
    bands = lax.axis_size("row")
    piece = rows // lax.axis_size(("col", "sub"))
    local, count, block = h_real.shape[0], h_real.shape[1], h_real.shape[2]
    order = bands * rows
    r = lax.axis_index("row")
    q = lax.axis_index(("col", "sub"))
    me_plane = lax.axis_index(("runs", "col"))
    me_core = lax.axis_index("sub")
    shares = lax.axis_size(("runs", "col", "sub"))
    per = 2 * local * count // shares
    dims = (bands, rows, cols, piece, local, count, block, per)

    smem = pl.BlockSpec(memory_space=pltpu.SMEM)
    vmem = pl.BlockSpec(memory_space=pltpu.VMEM)
    start = q * per
    share = jnp.where(
        lax.axis_index("runs") == 0,
        lax.dynamic_slice_in_dim(h_real.reshape(local * count, block, block), start, per, 0),
        lax.dynamic_slice_in_dim(h_imag.reshape(local * count, block, block), start, per, 0),
    ).reshape(per * block, block)
    col_rows = jnp.pad(h_cols.astype(BF16), ((0, 16 - local), (0, block - count)))
    message = jnp.concatenate([share, col_rows], axis=0)
    mine = jnp.concatenate(
        [h.transpose(0, 2, 1, 3).reshape(local, block, count * block) for h in (h_imag, h_real)], axis=1
    )
    arrived = [exchange(message, "row", k) for k in range(1, bands)]
    all_cols = [
        a[per * block : per * block + local, :count].astype(jnp.int32).reshape(-1) for a in [message] + arrived
    ]
    facts = jnp.concatenate([jnp.stack([r, q, me_plane, me_core]).astype(jnp.int32)] + all_cols)
    theirs = jnp.stack([a[: per * block] for a in arrived])
    near = jnp.stack([theirs] + [exchange(theirs, ("runs", "col"), k) for k in range(1, shares // 2)])
    rest = [exchange(here, "row", k) for k in range(1, bands)]
    far = exchange(near, "sub", 1)

    step = 2 * order * 2 * count * block * 2 * cols
    h_all, c_side = pl.pallas_call(
        functools.partial(powers_kernel, dims),
        out_shape=(
            jax.ShapeDtypeStruct((bands * local, 2 * block, count * block), BF16),
            jax.ShapeDtypeStruct((order, 6 * cols), BF16),
        ),
        in_specs=[smem] + [vmem] * 3,
        out_specs=(vmem, vmem),
        scratch_shapes=[
            pltpu.VMEM((order, cols), BF16),
            pltpu.VMEM((order, 2 * cols), BF16),
            pltpu.VMEM((order, 2 * cols), BF16),
            pltpu.VMEM((order, 2 * cols), F32),
        ],
        compiler_params=pltpu.CompilerParams(vmem_limit_bytes=POWERS_VMEM),
        cost_estimate=pl.CostEstimate(flops=5 * step // 2, bytes_accessed=2**20, transcendentals=0),
        name="powers",
    )(facts, mine, near, far)
    own, keep, send = pl.pallas_call(
        functools.partial(main_kernel, dims),
        out_shape=(
            jax.ShapeDtypeStruct((rows, cols), F32),
            jax.ShapeDtypeStruct((rows, cols), F32),
            jax.ShapeDtypeStruct((2, rows, cols), BF16),
        ),
        in_specs=[smem] + [vmem] * (bands + 2),
        out_specs=(vmem, vmem, vmem),
        scratch_shapes=[
            pltpu.VMEM((order, 2 * cols), BF16),
            pltpu.VMEM((order, 2 * cols), BF16),
            pltpu.VMEM((order, 2 * cols), BF16),
            pltpu.VMEM((order, 2 * piece), F32),
            pltpu.VMEM((rows, 2 * cols), F32),
            pltpu.VMEM((2, rows, 12 * cols), BF16),
            pltpu.VMEM((bands, rows, rows), F32),
        ],
        compiler_params=pltpu.CompilerParams(vmem_limit_bytes=MAIN_VMEM),
        cost_estimate=pl.CostEstimate(flops=5 * step, bytes_accessed=2**20, transcendentals=0),
        name="main",
    )(facts, here, *rest, h_all, c_side)
    swapped = exchange(send, "sub", 1)
    across = exchange((keep + swapped[1].astype(F32)).astype(BF16), "col", 1)
    total = here.astype(F32) + own + swapped[0].astype(F32) + across.astype(F32)
    return total[None]


def can_gather(mesh, local_packed, local_h):
    bands = mesh.shape["row"]
    rows, cols = local_packed[1], local_packed[2]
    local, count, block = local_h[0], local_h[1], local_h[2]
    shares = mesh.shape["runs"] * mesh.shape["col"] * mesh.shape["sub"]
    return (
        bands & (bands - 1) == 0
        and mesh.shape["runs"] == mesh.shape["col"] == mesh.shape["sub"] == 2
        and rows == cols == local * block
        and (2 * local * count) % shares == 0
        and local <= 16
        and count <= block
        and 80 * bands * rows * bands * rows // 2 <= VMEM_BYTES
    )


def body(mesh, packed, h_real, h_imag, h_cols):
    if can_gather(mesh, packed.shape, h_real.shape):
        return gathered_body(packed, h_real, h_imag, h_cols)
    return banded_body(packed, h_real, h_imag, h_cols)


def solution(mesh):
    in_specs = (
        P(("col", "sub"), ("runs", "row"), None),
        P("row", None, None, None),
        P("row", None, None, None),
        P("row", None),
    )
    out_specs = P(("col", "sub"), ("runs", "row"), None)
    return jax.shard_map(
        functools.partial(body, mesh), mesh=mesh, in_specs=in_specs, out_specs=out_specs, check_vma=False
    )
```

```python
import functools

import jax
import jax.numpy as jnp
from jax import lax
from jax.experimental import pallas as pl
from jax.experimental.pallas import tpu as pltpu
from jax.sharding import PartitionSpec as P

TERMS = 3


step_size = 0.5


def extended(block, sides, width):
    for axis, dim in sides:
        count = lax.axis_size(axis)
        forward = [(i, i + 1) for i in range(count - 1)]
        forward.append((count - 1, 0))
        backward = [(target, source) for source, target in forward]
        low = lax.ppermute(
            lax.slice_in_dim(block, block.shape[dim] - width, None, axis=dim), axis, forward
        )
        high = lax.ppermute(lax.slice_in_dim(block, 0, width, axis=dim), axis, backward)
        block = jnp.concatenate([low, block, high], axis=dim)
    return block


def mirror(stacked):
    groups, rows_here, col_count = stacked.shape
    piece_count = lax.axis_size(("col", "sub"))
    band_count = lax.axis_size("row")
    piece_len = rows_here // piece_count
    split_rows = stacked.reshape(groups, piece_count, piece_len, col_count)
    arrived = lax.all_to_all(split_rows, ("col", "sub"), split_axis=1, concat_axis=1, tiled=True)
    turned = jnp.swapaxes(arrived.reshape(groups, rows_here, col_count), 1, 2).reshape(
        groups, band_count, piece_len, rows_here
    )
    landed = lax.all_to_all(turned, "row", split_axis=1, concat_axis=1, tiled=True)
    spread = landed.reshape(groups, band_count, piece_len, piece_count, piece_len)
    placed = jnp.transpose(spread, (0, 3, 2, 1, 4))
    return placed.reshape(groups, rows_here, col_count)


def banded_body(packed, h_real, h_imag, h_cols):
    packed_here = packed.reshape(packed.shape[1], packed.shape[2])
    rows_here, col_count = packed_here.shape
    band_index = lax.axis_index("row")
    piece_index = lax.axis_index(("col", "sub"))
    piece_len = rows_here // lax.axis_size(("col", "sub"))
    flipped = mirror(packed_here[None])[0]
    row_ids = band_index * rows_here + jnp.arange(rows_here, dtype=jnp.int32)[:, None]
    col_local = jnp.arange(col_count, dtype=jnp.int32)[None, :]
    col_ids = col_local // piece_len * rows_here + piece_index * piece_len + col_local % piece_len
    upper_mask = row_ids <= col_ids
    real_part = jnp.where(upper_mask, packed_here, flipped)
    imag_part = jnp.where(
        row_ids > col_ids,
        packed_here,
        jnp.where(row_ids < col_ids, -flipped, jnp.zeros_like(flipped)),
    )
    current = jnp.stack([real_part, imag_part])
    summed = current.astype(jnp.float32)
    combined = jnp.stack([jnp.stack([h_imag, h_real], 2), jnp.stack([-h_real, h_imag], 2)])
    local_blocks = h_real.shape[0]
    block_len = h_real.shape[2]
    block_total = lax.axis_size("row") * local_blocks
    block_ids = band_index * local_blocks + jnp.arange(local_blocks, dtype=jnp.int32)[:, None]
    offsets = (h_cols - block_ids + 2) % block_total - 2
    starts = (
        (jnp.arange(local_blocks, dtype=jnp.int32)[:, None] + offsets + 2) * block_len
    ).reshape(-1)
    for term_index in range(1, TERMS + 1):
        padded = extended(current, (("row", 1),), 2 * block_len)
        sliced = jnp.stack(
            [
                lax.dynamic_slice_in_dim(padded, starts[k], block_len, 1)
                for k in range(starts.shape[0])
            ]
        )
        gathered = sliced.reshape(local_blocks, 4, 2, block_len, col_count)
        product = jnp.einsum(
            "obsgij,bsgjc->obic", combined, gathered, preferred_element_type=jnp.float32
        )
        generator = product.reshape(2, rows_here, col_count).astype(jnp.bfloat16)
        mirror_part = mirror(generator).astype(jnp.float32)
        own_part = generator.astype(jnp.float32)
        update = (
            step_size
            / term_index
            * jnp.stack([own_part[0] + mirror_part[0], own_part[1] - mirror_part[1]])
        )
        summed = summed + update
        current = update.astype(jnp.bfloat16)
    result = jnp.where(upper_mask, summed[0], summed[1])
    return result[None]


VMEM_BYTES = 56 * 2**20
POWERS_VMEM = 20 * 2**20
MAIN_VMEM = 22 * 2**20
OWN_VMEM = 14 * 2**20
F32 = jnp.float32
BF16 = jnp.bfloat16


def exchange(block, axes, offset):
    count = lax.axis_size(axes)
    return lax.ppermute(block, axes, [(i, i ^ offset) for i in range(count)])


def block_product(dims, facts, h_ref, at, take):
    bands, rows, cols, piece, local, count, block, per = dims
    starts = []
    for s in range(count):
        column = facts[4 + at * count + s]
        slot = lax.bitwise_xor(column // local, facts[0])
        starts.append(pl.multiple_of((slot * local + column % local) * block, block))
    right = jnp.concatenate([take(pl.ds(start, block)) for start in starts], axis=0)
    return jnp.dot(h_ref[at], right, preferred_element_type=F32)


def apply_a(dims, facts, h_ref, at, take, width):
    block = dims[6]
    got = block_product(dims, facts, h_ref, at, take)
    real = got[:block, :width] + got[block:, width:]
    imag = got[:block, width:] - got[block:, :width]
    return 0.5 * jnp.concatenate([real, imag], axis=1)


def powers_kernel(dims, facts, mine_ref, near_ref, far_ref, h_ref, c_ref, sel, c1_ref, c2_ref, csum):
    bands, rows, cols, piece, local, count, block, per = dims
    r, q, me_plane, me_core = facts[0], facts[1], facts[2], facts[3]
    h_ref[0:local] = mine_ref[...]
    for n in range(2 * near_ref.shape[0]):
        part = (near_ref, far_ref)[n % 2]
        share = lax.bitwise_xor(me_plane, n // 2) * 2 + lax.bitwise_xor(me_core, n % 2)
        for at in range(per):
            flat = share * per + at
            below = pl.multiple_of((1 - flat // (local * count)) * block, block)
            b = flat // count % local
            beside = pl.multiple_of(flat % count * block, block)
            for k in range(1, bands):
                h_ref[k * local + b, pl.ds(below, block), pl.ds(beside, block)] = part[
                    n // 2, k - 1, at * block : (at + 1) * block, :
                ]
    row_iota = lax.broadcasted_iota(jnp.int32, (rows, cols), 0)
    col_iota = lax.broadcasted_iota(jnp.int32, (rows, cols), 1)
    for k in range(bands):
        hit = (col_iota // piece == k) & (row_iota == q * piece + col_iota % piece)
        sel[k * rows : (k + 1) * rows, :] = jnp.where(hit, 1.0, 0.0).astype(BF16)

    def put_d(span, m, value):
        low = value.astype(BF16)
        c_ref[span, m * cols : (m + 1) * cols] = low[:, :cols]
        c_ref[span, (m + 3) * cols : (m + 4) * cols] = low[:, cols:]

    for at in range(bands * local):
        span = slice(at * block, (at + 1) * block)
        got = block_product(dims, facts, h_ref, at, lambda where: sel[where, :])
        c1 = 0.5 * jnp.concatenate([got[:block], -got[block:]], axis=1)
        c1_ref[span, :] = c1.astype(BF16)
        csum[span, :] = c1
        put_d(span, 2, 0.5 * c1)
    for at in range(bands * local):
        span = slice(at * block, (at + 1) * block)
        c2 = apply_a(dims, facts, h_ref, at, lambda where: c1_ref[where, :], cols)
        c2_ref[span, :] = c2.astype(BF16)
        both = csum[span, :] + 0.5 * c2
        csum[span, :] = both
        put_d(span, 1, both)
    for at in range(bands * local):
        span = slice(at * block, (at + 1) * block)
        c3 = apply_a(dims, facts, h_ref, at, lambda where: c2_ref[where, :], cols)
        put_d(span, 0, csum[span, :] + c3 * (1.0 / 6.0))


def swap_groups(value, r, piece):
    size = value.shape[1]
    groups = size // piece
    bit = 1
    while bit < groups:
        moved = jnp.concatenate(
            [value[:, (g ^ bit) * piece : (g ^ bit) * piece + piece] for g in range(groups)], axis=1
        )
        value = jnp.where(lax.bitwise_and(r, bit) != 0, moved, value)
        bit *= 2
    return value


def products(dims, facts, wanted, c_ref, n_ref, v1_ref, v2_ref, left, slab, outs):
    bands, rows, cols, piece, local, count, block, per = dims
    r, q = facts[0], facts[1]
    nt = (((1,), (1,)), ((), ()))
    size = len(wanted) * piece
    spans = [
        [pl.ds(pl.multiple_of(k * rows + p * piece, piece), piece) for p in wanted] for k in range(bands)
    ]
    i_own = lax.broadcasted_iota(jnp.int32, (piece, rows), 1)
    j_own = lax.broadcasted_iota(jnp.int32, (piece, rows), 0)
    upper = jnp.concatenate([i_own <= p * piece + j_own for p in wanted], axis=0)
    mine = lax.broadcasted_iota(jnp.int32, (size, rows), 1) // piece == q

    def against(which, slots):
        right = jnp.concatenate(
            [
                jnp.concatenate([ref[span, :] for ref in (c_ref, n_ref, v1_ref, v2_ref)], axis=1)
                for k in slots
                for span in spans[k]
            ],
            axis=0,
        )
        return lax.dot_general(right, left[which], nt, preferred_element_type=F32)

    for k in range(0, bands, 2):
        if k == 0:
            next_side = (lax.bitwise_xor(r, 1) < r).astype(jnp.int32)
            got = [jnp.where(upper, against(0, (0,)), against(1, (0,))), against(next_side, (1,))]
        else:
            side = against((lax.bitwise_xor(r, k) < r).astype(jnp.int32), (k, k + 1))
            got = [side[:size], side[size:]]
        for n in (0, 1):
            thin = jnp.concatenate([slab[span, :] for span in spans[k + n]], axis=0)
            real = jnp.concatenate([thin[:, :piece]] * (rows // piece), axis=1)
            imag = jnp.concatenate([-thin[:, piece:]] * (rows // piece), axis=1)
            above = upper if k + n == 0 else lax.bitwise_xor(r, k + n) > r
            outs[k + n] = got[n] + jnp.where(mine, jnp.where(above, real, imag), 0.0)

    def target(n):
        return jnp.concatenate(
            [outs[lax.bitwise_xor(r, b), n * piece : (n + 1) * piece, :] for b in range(bands)], axis=0
        ).T

    return target


def main_kernel(dims, facts, *refs):
    bands, rows, cols, piece, local, count, block, per = dims
    f_refs = refs[:bands]
    h_ref, c_ref, keep_ref, send_ref, n_ref, v1_ref, v2_ref, left, slab, tops, outs = refs[bands:]
    r, q = facts[0], facts[1]
    row_iota = lax.broadcasted_iota(jnp.int32, (rows, cols), 0)
    col_iota = lax.broadcasted_iota(jnp.int32, (rows, cols), 1)
    col_abs = col_iota // piece * rows + q * piece + col_iota % piece
    for k in range(bands):
        here = f_refs[-k % bands][...].astype(F32)
        row_abs = lax.bitwise_xor(r, k) * rows + row_iota
        real = jnp.where(row_abs < col_abs, here, jnp.where(row_abs == col_abs, 0.5 * here, 0.0))
        imag = jnp.where(row_abs > col_abs, here, 0.0)
        for half, value in enumerate((real, imag)):
            n_ref[k * rows : (k + 1) * rows, half * cols : (half + 1) * cols] = swap_groups(
                value, r, piece
            ).astype(BF16)

    def thin(value):
        return jnp.concatenate([value[:, :piece], value[:, cols : cols + piece]], axis=1)

    for at in range(bands * local):
        span = slice(at * block, (at + 1) * block)
        v1 = apply_a(dims, facts, h_ref, at, lambda where: n_ref[where, :], cols)
        v1_ref[span, :] = v1.astype(BF16)
        slab[span, :] = thin(v1)
        if at < local:
            tops[span, :] = v1
    for at in range(bands * local):
        span = slice(at * block, (at + 1) * block)
        v2 = apply_a(dims, facts, h_ref, at, lambda where: v1_ref[where, :], cols)
        v2_ref[span, :] = v2.astype(BF16)
        slab[span, :] += 0.5 * thin(v2)
        if at < local:
            tops[span, :] += 0.5 * v2
    for at in range(bands * local):
        span = slice(at * block, (at + 1) * block)
        if at < local:
            v3 = apply_a(dims, facts, h_ref, at, lambda where: v2_ref[where, :], cols)
            tops[span, :] += v3 * (1.0 / 6.0)
            slab[span, :] += thin(v3) * (1.0 / 6.0)
        else:
            v3 = apply_a(
                dims,
                facts,
                h_ref,
                at,
                lambda where: jnp.concatenate(
                    [v2_ref[where, 0:piece], v2_ref[where, cols : cols + piece]],
                    axis=1,
                ),
                piece,
            )
            slab[span, :] += v3 * (1.0 / 6.0)
    own = slice(0, rows)
    three = 3 * cols
    for m, t_ref in enumerate((n_ref, v1_ref, v2_ref)):
        tr, ti = t_ref[own, :cols], t_ref[own, cols:]
        cr = c_ref[own, m * cols : (m + 1) * cols]
        ci = c_ref[own, three + m * cols : three + (m + 1) * cols]
        for which, (first, second, third, fourth) in enumerate(((tr, ti, cr, ci), (ti, -tr, ci, -cr))):
            left[which, :, m * cols : (m + 1) * cols] = first
            left[which, :, three + m * cols : three + (m + 1) * cols] = second
            left[which, :, 2 * three + 2 * m * cols : 2 * three + (2 * m + 1) * cols] = third
            left[which, :, 2 * three + (2 * m + 1) * cols : 2 * three + (2 * m + 2) * cols] = fourth
    far = lax.bitwise_xor(q, 2)
    wanted = (lax.bitwise_xor(far, 1), lax.bitwise_xor(q, 1), far)
    target = products(dims, facts, wanted, c_ref, n_ref, v1_ref, v2_ref, left, slab, outs)
    send_ref[0] = target(0).astype(BF16)
    send_ref[1] = target(1).astype(BF16)
    keep_ref[...] = target(2)


def own_kernel(dims, facts, c_ref, n_ref, v1_ref, v2_ref, left, slab, tops, own_ref, outs):
    bands, rows, cols, piece, local, count, block, per = dims
    r, q = facts[0], facts[1]
    target = products(dims, facts, (q,), c_ref, n_ref, v1_ref, v2_ref, left, slab, outs)
    col_iota = lax.broadcasted_iota(jnp.int32, (rows, cols), 1)
    col_abs = col_iota // piece * rows + q * piece + col_iota % piece
    row_abs = r * rows + lax.broadcasted_iota(jnp.int32, (rows, cols), 0)
    real = swap_groups(tops[:, :cols], r, piece)
    imag = swap_groups(tops[:, cols:], r, piece)
    own_ref[...] = target(0) + jnp.where(row_abs <= col_abs, real, imag)


def gathered_body(packed, h_real, h_imag, h_cols):
    here = packed.reshape(packed.shape[1], packed.shape[2])
    rows, cols = here.shape
    bands = lax.axis_size("row")
    piece = rows // lax.axis_size(("col", "sub"))
    local, count, block = h_real.shape[0], h_real.shape[1], h_real.shape[2]
    order = bands * rows
    r = lax.axis_index("row")
    q = lax.axis_index(("col", "sub"))
    me_plane = lax.axis_index(("runs", "col"))
    me_core = lax.axis_index("sub")
    shares = lax.axis_size(("runs", "col", "sub"))
    per = 2 * local * count // shares
    dims = (bands, rows, cols, piece, local, count, block, per)

    smem = pl.BlockSpec(memory_space=pltpu.SMEM)
    vmem = pl.BlockSpec(memory_space=pltpu.VMEM)
    start = q * per
    share = jnp.where(
        lax.axis_index("runs") == 0,
        lax.dynamic_slice_in_dim(h_real.reshape(local * count, block, block), start, per, 0),
        lax.dynamic_slice_in_dim(h_imag.reshape(local * count, block, block), start, per, 0),
    ).reshape(per * block, block)
    col_rows = jnp.pad(h_cols.astype(BF16), ((0, 16 - local), (0, block - count)))
    message = jnp.concatenate([share, col_rows], axis=0)
    mine = jnp.concatenate(
        [h.transpose(0, 2, 1, 3).reshape(local, block, count * block) for h in (h_imag, h_real)], axis=1
    )
    arrived = [exchange(message, "row", k) for k in range(1, bands)]
    all_cols = [
        a[per * block : per * block + local, :count].astype(jnp.int32).reshape(-1) for a in [message] + arrived
    ]
    facts = jnp.concatenate([jnp.stack([r, q, me_plane, me_core]).astype(jnp.int32)] + all_cols)
    theirs = jnp.stack([a[: per * block] for a in arrived])
    near = jnp.stack([theirs] + [exchange(theirs, ("runs", "col"), k) for k in range(1, shares // 2)])
    rest = [exchange(here, "row", k) for k in range(bands - 1, 0, -1)]
    far = exchange(near, "sub", 1)

    step = 2 * order * 2 * count * block * 2 * cols
    h_all, c_side = pl.pallas_call(
        functools.partial(powers_kernel, dims),
        out_shape=(
            jax.ShapeDtypeStruct((bands * local, 2 * block, count * block), BF16),
            jax.ShapeDtypeStruct((order, 6 * cols), BF16),
        ),
        in_specs=[smem] + [vmem] * 3,
        out_specs=(vmem, vmem),
        scratch_shapes=[
            pltpu.VMEM((order, cols), BF16),
            pltpu.VMEM((order, 2 * cols), BF16),
            pltpu.VMEM((order, 2 * cols), BF16),
            pltpu.VMEM((order, 2 * cols), F32),
        ],
        compiler_params=pltpu.CompilerParams(vmem_limit_bytes=POWERS_VMEM),
        cost_estimate=pl.CostEstimate(flops=5 * step // 2, bytes_accessed=2**20, transcendentals=0),
        name="powers",
    )(facts, mine, near, far)
    block_shape = jax.ShapeDtypeStruct((rows, cols), F32)
    v_shape = jax.ShapeDtypeStruct((order, 2 * cols), BF16)
    keep, send, *state = pl.pallas_call(
        functools.partial(main_kernel, dims),
        out_shape=(
            block_shape,
            jax.ShapeDtypeStruct((2, rows, cols), BF16),
            v_shape,
            v_shape,
            v_shape,
            jax.ShapeDtypeStruct((2, rows, 12 * cols), BF16),
            jax.ShapeDtypeStruct((order, 2 * piece), F32),
            jax.ShapeDtypeStruct((rows, 2 * cols), F32),
        ),
        in_specs=[smem] + [vmem] * (bands + 2),
        out_specs=(vmem,) * 8,
        scratch_shapes=[pltpu.VMEM((bands, 3 * piece, rows), F32)],
        compiler_params=pltpu.CompilerParams(vmem_limit_bytes=MAIN_VMEM),
        cost_estimate=pl.CostEstimate(flops=4 * step, bytes_accessed=2**20, transcendentals=0),
        name="main",
    )(facts, here, *rest, h_all, c_side)
    swapped = exchange(send, "sub", 1)
    across = exchange((keep + swapped[0].astype(F32)).astype(BF16), "col", 1)
    own = pl.pallas_call(
        functools.partial(own_kernel, dims),
        out_shape=block_shape,
        in_specs=[smem] + [vmem] * 7,
        out_specs=vmem,
        scratch_shapes=[pltpu.VMEM((bands, piece, rows), F32)],
        compiler_params=pltpu.CompilerParams(vmem_limit_bytes=OWN_VMEM),
        cost_estimate=pl.CostEstimate(flops=step, bytes_accessed=2**20, transcendentals=0),
        name="own",
    )(facts, c_side, *state)
    total = here.astype(F32) + own + swapped[1].astype(F32) + across.astype(F32)
    return total[None]


def can_gather(mesh, local_packed, local_h):
    bands = mesh.shape["row"]
    rows, cols = local_packed[1], local_packed[2]
    local, count, block = local_h[0], local_h[1], local_h[2]
    shares = mesh.shape["runs"] * mesh.shape["col"] * mesh.shape["sub"]
    return (
        bands & (bands - 1) == 0
        and bands > 1
        and mesh.shape["runs"] == mesh.shape["col"] == mesh.shape["sub"] == 2
        and rows == cols == local * block
        and (2 * local * count) % shares == 0
        and local <= 16
        and count <= block
        and 80 * bands * rows * bands * rows // 2 <= VMEM_BYTES
    )


def body(mesh, packed, h_real, h_imag, h_cols):
    if can_gather(mesh, packed.shape, h_real.shape):
        return gathered_body(packed, h_real, h_imag, h_cols)
    return banded_body(packed, h_real, h_imag, h_cols)


def solution(mesh):
    in_specs = (
        P(("col", "sub"), ("runs", "row"), None),
        P("row", None, None, None),
        P("row", None, None, None),
        P("row", None),
    )
    out_specs = P(("col", "sub"), ("runs", "row"), None)
    return jax.shard_map(
        functools.partial(body, mesh), mesh=mesh, in_specs=in_specs, out_specs=out_specs, check_vma=False
    )
```

```python
import functools

import jax
import jax.numpy as jnp
from jax import lax
from jax.experimental import pallas as pl
from jax.experimental.pallas import tpu as pltpu
from jax.sharding import PartitionSpec as P

TERMS = 3


step_size = 0.5


def extended(block, sides, width):
    for axis, dim in sides:
        count = lax.axis_size(axis)
        forward = [(i, i + 1) for i in range(count - 1)]
        forward.append((count - 1, 0))
        backward = [(target, source) for source, target in forward]
        low = lax.ppermute(
            lax.slice_in_dim(block, block.shape[dim] - width, None, axis=dim), axis, forward
        )
        high = lax.ppermute(lax.slice_in_dim(block, 0, width, axis=dim), axis, backward)
        block = jnp.concatenate([low, block, high], axis=dim)
    return block


def mirror(stacked):
    groups, rows_here, col_count = stacked.shape
    piece_count = lax.axis_size(("col", "sub"))
    band_count = lax.axis_size("row")
    piece_len = rows_here // piece_count
    split_rows = stacked.reshape(groups, piece_count, piece_len, col_count)
    arrived = lax.all_to_all(split_rows, ("col", "sub"), split_axis=1, concat_axis=1, tiled=True)
    turned = jnp.swapaxes(arrived.reshape(groups, rows_here, col_count), 1, 2).reshape(
        groups, band_count, piece_len, rows_here
    )
    landed = lax.all_to_all(turned, "row", split_axis=1, concat_axis=1, tiled=True)
    spread = landed.reshape(groups, band_count, piece_len, piece_count, piece_len)
    placed = jnp.transpose(spread, (0, 3, 2, 1, 4))
    return placed.reshape(groups, rows_here, col_count)


def banded_body(packed, h_real, h_imag, h_cols):
    packed_here = packed.reshape(packed.shape[1], packed.shape[2])
    rows_here, col_count = packed_here.shape
    band_index = lax.axis_index("row")
    piece_index = lax.axis_index(("col", "sub"))
    piece_len = rows_here // lax.axis_size(("col", "sub"))
    flipped = mirror(packed_here[None])[0]
    row_ids = band_index * rows_here + jnp.arange(rows_here, dtype=jnp.int32)[:, None]
    col_local = jnp.arange(col_count, dtype=jnp.int32)[None, :]
    col_ids = col_local // piece_len * rows_here + piece_index * piece_len + col_local % piece_len
    upper_mask = row_ids <= col_ids
    real_part = jnp.where(upper_mask, packed_here, flipped)
    imag_part = jnp.where(
        row_ids > col_ids,
        packed_here,
        jnp.where(row_ids < col_ids, -flipped, jnp.zeros_like(flipped)),
    )
    current = jnp.stack([real_part, imag_part])
    summed = current.astype(jnp.float32)
    combined = jnp.stack([jnp.stack([h_imag, h_real], 2), jnp.stack([-h_real, h_imag], 2)])
    local_blocks = h_real.shape[0]
    block_len = h_real.shape[2]
    block_total = lax.axis_size("row") * local_blocks
    block_ids = band_index * local_blocks + jnp.arange(local_blocks, dtype=jnp.int32)[:, None]
    offsets = (h_cols - block_ids + 2) % block_total - 2
    starts = (
        (jnp.arange(local_blocks, dtype=jnp.int32)[:, None] + offsets + 2) * block_len
    ).reshape(-1)
    for term_index in range(1, TERMS + 1):
        padded = extended(current, (("row", 1),), 2 * block_len)
        sliced = jnp.stack(
            [
                lax.dynamic_slice_in_dim(padded, starts[k], block_len, 1)
                for k in range(starts.shape[0])
            ]
        )
        gathered = sliced.reshape(local_blocks, 4, 2, block_len, col_count)
        product = jnp.einsum(
            "obsgij,bsgjc->obic", combined, gathered, preferred_element_type=jnp.float32
        )
        generator = product.reshape(2, rows_here, col_count).astype(jnp.bfloat16)
        mirror_part = mirror(generator).astype(jnp.float32)
        own_part = generator.astype(jnp.float32)
        update = (
            step_size
            / term_index
            * jnp.stack([own_part[0] + mirror_part[0], own_part[1] - mirror_part[1]])
        )
        summed = summed + update
        current = update.astype(jnp.bfloat16)
    result = jnp.where(upper_mask, summed[0], summed[1])
    return result[None]


VMEM_BYTES = 56 * 2**20
NEAR_VMEM = 8 * 2**20
POWERS_VMEM = 20 * 2**20
MAIN_VMEM = 22 * 2**20
OWN_VMEM = 14 * 2**20
F32 = jnp.float32
BF16 = jnp.bfloat16


def exchange(block, axes, offset):
    count = lax.axis_size(axes)
    return lax.ppermute(block, axes, [(i, i ^ offset) for i in range(count)])


def block_product(dims, facts, h_refs, at, take):
    bands, rows, cols, piece, local, count, block, per = dims
    starts = []
    for side in (0, 1):
        for a in range(per):
            s = lax.bitwise_xor(facts[3], side) * per + a
            column = facts[4 + at * count + s]
            slot = lax.bitwise_xor(column // local, facts[0])
            starts.append(pl.multiple_of((slot * local + column % local) * block, block))
    right = jnp.concatenate([take(pl.ds(start, block)) for start in starts], axis=0)
    return jnp.dot(
        jnp.concatenate([ref[at] for ref in h_refs], axis=1), right, preferred_element_type=F32
    )


def apply_a(dims, facts, h_refs, at, take, width):
    block = dims[6]
    got = block_product(dims, facts, h_refs, at, take)
    real = got[:block, :width] + got[block:, width:]
    imag = got[:block, width:] - got[block:, :width]
    return 0.5 * jnp.concatenate([real, imag], axis=1)


def place_side(dims, facts, side, mine_ref, part_ref, h_ref):
    bands, rows, cols, piece, local, count, block, per = dims
    core = lax.bitwise_xor(facts[3], side)
    wide = per * block
    for b in range(local):
        h_ref[b] = mine_ref[b, :, pl.ds(pl.multiple_of(core * wide, wide), wide)]
    for n in range(part_ref.shape[0]):
        flat = (lax.bitwise_xor(facts[2], n) * 2 + core) * per
        below = pl.ds(pl.multiple_of((1 - flat // (local * count)) * block, block), block)
        b = flat // count % local
        for k in range(1, bands):
            for at in range(per):
                h_ref[k * local + b, below, at * block : (at + 1) * block] = part_ref[
                    n, k - 1, at * block : (at + 1) * block, :
                ]


def near_kernel(dims, facts, mine_ref, near_ref, h_ref, sel_ref):
    bands, rows, cols, piece, local, count, block, per = dims
    place_side(dims, facts, 0, mine_ref, near_ref, h_ref)
    row_iota = lax.broadcasted_iota(jnp.int32, (rows, cols), 0)
    col_iota = lax.broadcasted_iota(jnp.int32, (rows, cols), 1)
    for k in range(bands):
        hit = (col_iota // piece == k) & (row_iota == facts[1] * piece + col_iota % piece)
        sel_ref[k * rows : (k + 1) * rows, :] = jnp.where(hit, 1.0, 0.0).astype(BF16)


def powers_kernel(dims, facts, mine_ref, far_ref, near_h, sel, far_h, c_ref, c1_ref, c2_ref, csum):
    bands, rows, cols, piece, local, count, block, per = dims
    place_side(dims, facts, 1, mine_ref, far_ref, far_h)
    h_refs = (near_h, far_h)

    def put_d(span, m, value):
        low = value.astype(BF16)
        c_ref[span, m * cols : (m + 1) * cols] = low[:, :cols]
        c_ref[span, (m + 3) * cols : (m + 4) * cols] = low[:, cols:]

    for at in range(bands * local):
        span = slice(at * block, (at + 1) * block)
        got = block_product(dims, facts, h_refs, at, lambda where: sel[where, :])
        c1 = 0.5 * jnp.concatenate([got[:block], -got[block:]], axis=1)
        c1_ref[span, :] = c1.astype(BF16)
        csum[span, :] = c1
        put_d(span, 2, 0.5 * c1)
    for at in range(bands * local):
        span = slice(at * block, (at + 1) * block)
        c2 = apply_a(dims, facts, h_refs, at, lambda where: c1_ref[where, :], cols)
        c2_ref[span, :] = c2.astype(BF16)
        both = csum[span, :] + 0.5 * c2
        csum[span, :] = both
        put_d(span, 1, both)
    for at in range(bands * local):
        span = slice(at * block, (at + 1) * block)
        c3 = apply_a(dims, facts, h_refs, at, lambda where: c2_ref[where, :], cols)
        put_d(span, 0, csum[span, :] + c3 * (1.0 / 6.0))


def swap_groups(value, r, piece):
    size = value.shape[1]
    groups = size // piece
    bit = 1
    while bit < groups:
        moved = jnp.concatenate(
            [value[:, (g ^ bit) * piece : (g ^ bit) * piece + piece] for g in range(groups)], axis=1
        )
        value = jnp.where(lax.bitwise_and(r, bit) != 0, moved, value)
        bit *= 2
    return value


def products(dims, facts, wanted, c_ref, n_ref, v1_ref, v2_ref, left, slab, outs):
    bands, rows, cols, piece, local, count, block, per = dims
    r, q = facts[0], facts[1]
    nt = (((1,), (1,)), ((), ()))
    size = len(wanted) * piece
    spans = [
        [pl.ds(pl.multiple_of(k * rows + p * piece, piece), piece) for p in wanted] for k in range(bands)
    ]
    i_own = lax.broadcasted_iota(jnp.int32, (piece, rows), 1)
    j_own = lax.broadcasted_iota(jnp.int32, (piece, rows), 0)
    upper = jnp.concatenate([i_own <= p * piece + j_own for p in wanted], axis=0)
    mine = lax.broadcasted_iota(jnp.int32, (size, rows), 1) // piece == q

    def against(which, slots):
        right = jnp.concatenate(
            [
                jnp.concatenate([ref[span, :] for ref in (c_ref, n_ref, v1_ref, v2_ref)], axis=1)
                for k in slots
                for span in spans[k]
            ],
            axis=0,
        )
        return lax.dot_general(right, left[which], nt, preferred_element_type=F32)

    for k in range(0, bands, 2):
        if k == 0:
            next_side = (lax.bitwise_xor(r, 1) < r).astype(jnp.int32)
            got = [jnp.where(upper, against(0, (0,)), against(1, (0,))), against(next_side, (1,))]
        else:
            side = against((lax.bitwise_xor(r, k) < r).astype(jnp.int32), (k, k + 1))
            got = [side[:size], side[size:]]
        for n in (0, 1):
            thin = jnp.concatenate([slab[span, :] for span in spans[k + n]], axis=0)
            real = jnp.concatenate([thin[:, :piece]] * (rows // piece), axis=1)
            imag = jnp.concatenate([-thin[:, piece:]] * (rows // piece), axis=1)
            above = upper if k + n == 0 else lax.bitwise_xor(r, k + n) > r
            outs[k + n] = got[n] + jnp.where(mine, jnp.where(above, real, imag), 0.0)

    def target(n):
        return jnp.concatenate(
            [outs[lax.bitwise_xor(r, b), n * piece : (n + 1) * piece, :] for b in range(bands)], axis=0
        ).T

    return target


def main_kernel(dims, facts, *refs):
    bands, rows, cols, piece, local, count, block, per = dims
    f_refs = refs[:bands]
    near_h, far_h, c_ref, keep_ref, send_ref, n_ref, v1_ref, v2_ref, left, slab, tops, outs = refs[bands:]
    h_refs = (near_h, far_h)
    r, q = facts[0], facts[1]
    row_iota = lax.broadcasted_iota(jnp.int32, (rows, cols), 0)
    col_iota = lax.broadcasted_iota(jnp.int32, (rows, cols), 1)
    col_abs = lax.bitwise_xor(col_iota // piece, r) * rows + q * piece + col_iota % piece
    for k in range(bands):
        here = swap_groups(f_refs[-k % bands][...].astype(F32), r, piece)
        row_abs = lax.bitwise_xor(r, k) * rows + row_iota
        real = jnp.where(row_abs < col_abs, here, jnp.where(row_abs == col_abs, 0.5 * here, 0.0))
        imag = jnp.where(row_abs > col_abs, here, 0.0)
        n_ref[k * rows : (k + 1) * rows, :] = jnp.concatenate([real, imag], axis=1).astype(BF16)

    def thin(value):
        return jnp.concatenate([value[:, :piece], value[:, cols : cols + piece]], axis=1)

    for at in range(bands * local):
        span = slice(at * block, (at + 1) * block)
        v1 = apply_a(dims, facts, h_refs, at, lambda where: n_ref[where, :], cols)
        v1_ref[span, :] = v1.astype(BF16)
        slab[span, :] = thin(v1)
        if at < local:
            tops[span, :] = v1
    for at in range(bands * local):
        span = slice(at * block, (at + 1) * block)
        v2 = apply_a(dims, facts, h_refs, at, lambda where: v1_ref[where, :], cols)
        v2_ref[span, :] = v2.astype(BF16)
        slab[span, :] += 0.5 * thin(v2)
        if at < local:
            tops[span, :] += 0.5 * v2
    for at in range(bands * local):
        span = slice(at * block, (at + 1) * block)
        if at < local:
            v3 = apply_a(dims, facts, h_refs, at, lambda where: v2_ref[where, :], cols)
            tops[span, :] += v3 * (1.0 / 6.0)
            slab[span, :] += thin(v3) * (1.0 / 6.0)
        else:
            v3 = apply_a(
                dims,
                facts,
                h_refs,
                at,
                lambda where: jnp.concatenate(
                    [v2_ref[where, 0:piece], v2_ref[where, cols : cols + piece]],
                    axis=1,
                ),
                piece,
            )
            slab[span, :] += v3 * (1.0 / 6.0)
    own = slice(0, rows)
    three = 3 * cols
    for m, t_ref in enumerate((n_ref, v1_ref, v2_ref)):
        tr, ti = t_ref[own, :cols], t_ref[own, cols:]
        cr = c_ref[own, m * cols : (m + 1) * cols]
        ci = c_ref[own, three + m * cols : three + (m + 1) * cols]
        for which, (first, second, third, fourth) in enumerate(((tr, ti, cr, ci), (ti, -tr, ci, -cr))):
            left[which, :, m * cols : (m + 1) * cols] = first
            left[which, :, three + m * cols : three + (m + 1) * cols] = second
            left[which, :, 2 * three + 2 * m * cols : 2 * three + (2 * m + 1) * cols] = third
            left[which, :, 2 * three + (2 * m + 1) * cols : 2 * three + (2 * m + 2) * cols] = fourth
    far = lax.bitwise_xor(q, 2)
    wanted = (lax.bitwise_xor(far, 1), lax.bitwise_xor(q, 1), far)
    target = products(dims, facts, wanted, c_ref, n_ref, v1_ref, v2_ref, left, slab, outs)
    send_ref[0] = target(0).astype(BF16)
    send_ref[1] = target(1).astype(BF16)
    keep_ref[...] = target(2)


def own_kernel(dims, facts, c_ref, n_ref, v1_ref, v2_ref, left, slab, tops, own_ref, outs):
    bands, rows, cols, piece, local, count, block, per = dims
    r, q = facts[0], facts[1]
    target = products(dims, facts, (q,), c_ref, n_ref, v1_ref, v2_ref, left, slab, outs)
    col_iota = lax.broadcasted_iota(jnp.int32, (rows, cols), 1)
    col_abs = col_iota // piece * rows + q * piece + col_iota % piece
    row_abs = r * rows + lax.broadcasted_iota(jnp.int32, (rows, cols), 0)
    real = swap_groups(tops[:, :cols], r, piece)
    imag = swap_groups(tops[:, cols:], r, piece)
    own_ref[...] = target(0) + jnp.where(row_abs <= col_abs, real, imag)


def gathered_body(packed, h_real, h_imag, h_cols):
    here = packed.reshape(packed.shape[1], packed.shape[2])
    rows, cols = here.shape
    bands = lax.axis_size("row")
    piece = rows // lax.axis_size(("col", "sub"))
    local, count, block = h_real.shape[0], h_real.shape[1], h_real.shape[2]
    order = bands * rows
    r = lax.axis_index("row")
    q = lax.axis_index(("col", "sub"))
    me_plane = lax.axis_index(("runs", "col"))
    me_core = lax.axis_index("sub")
    shares = lax.axis_size(("runs", "col", "sub"))
    per = 2 * local * count // shares
    dims = (bands, rows, cols, piece, local, count, block, per)

    smem = pl.BlockSpec(memory_space=pltpu.SMEM)
    vmem = pl.BlockSpec(memory_space=pltpu.VMEM)
    flat_real, flat_imag = [h.reshape(local * count, block, block) for h in (h_real, h_imag)]

    def pick(first, second, at):
        return jnp.where(
            lax.axis_index("runs") == 0,
            lax.dynamic_slice_in_dim(first, at * per, per, 0),
            lax.dynamic_slice_in_dim(second, at * per, per, 0),
        ).reshape(per * block, block)

    size = per * block
    col_rows = jnp.pad(h_cols.astype(BF16), ((0, 16 - local), (0, block - count)))
    message = jnp.concatenate([pick(flat_real, flat_imag, q), col_rows], axis=0)
    diagonal = pick(flat_imag, flat_real, lax.bitwise_xor(q, 2))
    mine = jnp.concatenate(
        [h.transpose(0, 2, 1, 3).reshape(local, block, count * block) for h in (h_imag, h_real)], axis=1
    )
    arrived = [exchange(message, "row", k) for k in range(1, bands)]
    all_cols = [a[size : size + local, :count].astype(jnp.int32).reshape(-1) for a in [message] + arrived]
    facts = jnp.concatenate([jnp.stack([r, q, me_plane, me_core]).astype(jnp.int32)] + all_cols)
    theirs = lax.optimization_barrier(jnp.stack([a[:size] for a in arrived]))
    across_plane = jnp.concatenate([exchange(diagonal, "row", 1)[None], exchange(theirs[1:], ("runs", "col"), 3)], axis=0)
    near = jnp.stack([theirs] + [exchange(theirs, ("runs", "col"), k) for k in (1, 2)] + [across_plane])
    rest = [exchange(here, "row", k) for k in range(bands - 1, 0, -1)]
    far = exchange(near, "sub", 1)

    step = 2 * order * 2 * count * block * 2 * cols
    half_shape = jax.ShapeDtypeStruct((bands * local, 2 * block, per * block), BF16)
    near_h, sel = pl.pallas_call(
        functools.partial(near_kernel, dims),
        out_shape=(half_shape, jax.ShapeDtypeStruct((order, cols), BF16)),
        in_specs=[smem] + [vmem] * 2,
        out_specs=(vmem, vmem),
        compiler_params=pltpu.CompilerParams(vmem_limit_bytes=NEAR_VMEM),
        cost_estimate=pl.CostEstimate(flops=0, bytes_accessed=2**20, transcendentals=0),
        name="near",
    )(facts, mine, near)
    far_h, c_side = pl.pallas_call(
        functools.partial(powers_kernel, dims),
        out_shape=(half_shape, jax.ShapeDtypeStruct((order, 6 * cols), BF16)),
        in_specs=[smem] + [vmem] * 4,
        out_specs=(vmem, vmem),
        scratch_shapes=[
            pltpu.VMEM((order, 2 * cols), BF16),
            pltpu.VMEM((order, 2 * cols), BF16),
            pltpu.VMEM((order, 2 * cols), F32),
        ],
        compiler_params=pltpu.CompilerParams(vmem_limit_bytes=POWERS_VMEM),
        cost_estimate=pl.CostEstimate(flops=5 * step // 2, bytes_accessed=2**20, transcendentals=0),
        name="powers",
    )(facts, mine, far, near_h, sel)
    block_shape = jax.ShapeDtypeStruct((rows, cols), F32)
    v_shape = jax.ShapeDtypeStruct((order, 2 * cols), BF16)
    keep, send, *state = pl.pallas_call(
        functools.partial(main_kernel, dims),
        out_shape=(
            block_shape,
            jax.ShapeDtypeStruct((2, rows, cols), BF16),
            v_shape,
            v_shape,
            v_shape,
            jax.ShapeDtypeStruct((2, rows, 12 * cols), BF16),
            jax.ShapeDtypeStruct((order, 2 * piece), F32),
            jax.ShapeDtypeStruct((rows, 2 * cols), F32),
        ),
        in_specs=[smem] + [vmem] * (bands + 3),
        out_specs=(vmem,) * 8,
        scratch_shapes=[pltpu.VMEM((bands, 3 * piece, rows), F32)],
        compiler_params=pltpu.CompilerParams(vmem_limit_bytes=MAIN_VMEM),
        cost_estimate=pl.CostEstimate(flops=4 * step, bytes_accessed=2**20, transcendentals=0),
        name="main",
    )(facts, here, *rest, near_h, far_h, c_side)
    swapped = exchange(send, "sub", 1)
    across = exchange((keep + swapped[0].astype(F32)).astype(BF16), "col", 1)
    own = pl.pallas_call(
        functools.partial(own_kernel, dims),
        out_shape=block_shape,
        in_specs=[smem] + [vmem] * 7,
        out_specs=vmem,
        scratch_shapes=[pltpu.VMEM((bands, piece, rows), F32)],
        compiler_params=pltpu.CompilerParams(vmem_limit_bytes=OWN_VMEM),
        cost_estimate=pl.CostEstimate(flops=step, bytes_accessed=2**20, transcendentals=0),
        name="own",
    )(facts, c_side, *state)
    total = here.astype(F32) + own + swapped[1].astype(F32) + across.astype(F32)
    return total[None]


def can_gather(mesh, local_packed, local_h):
    bands = mesh.shape["row"]
    rows, cols = local_packed[1], local_packed[2]
    local, count, block = local_h[0], local_h[1], local_h[2]
    shares = mesh.shape["runs"] * mesh.shape["col"] * mesh.shape["sub"]
    return (
        bands & (bands - 1) == 0
        and bands > 2
        and mesh.shape["runs"] == mesh.shape["col"] == mesh.shape["sub"] == 2
        and rows == cols == local * block
        and (2 * local * count) % shares == 0
        and local <= 16
        and count * shares == 4 * local * count
        and count <= block
        and 80 * bands * rows * bands * rows // 2 <= VMEM_BYTES
    )


def body(mesh, packed, h_real, h_imag, h_cols):
    if can_gather(mesh, packed.shape, h_real.shape):
        return gathered_body(packed, h_real, h_imag, h_cols)
    return banded_body(packed, h_real, h_imag, h_cols)


def solution(mesh):
    in_specs = (
        P(("col", "sub"), ("runs", "row"), None),
        P("row", None, None, None),
        P("row", None, None, None),
        P("row", None),
    )
    out_specs = P(("col", "sub"), ("runs", "row"), None)
    return jax.shard_map(
        functools.partial(body, mesh), mesh=mesh, in_specs=in_specs, out_specs=out_specs, check_vma=False
    )
```

```python
import functools

import jax
import jax.numpy as jnp
from jax import lax
from jax.experimental import pallas as pl
from jax.experimental.pallas import tpu as pltpu
from jax.sharding import PartitionSpec as P

TERMS = 3


step_size = 0.5


def extended(block, sides, width):
    for axis, dim in sides:
        count = lax.axis_size(axis)
        forward = [(i, i + 1) for i in range(count - 1)]
        forward.append((count - 1, 0))
        backward = [(target, source) for source, target in forward]
        low = lax.ppermute(
            lax.slice_in_dim(block, block.shape[dim] - width, None, axis=dim), axis, forward
        )
        high = lax.ppermute(lax.slice_in_dim(block, 0, width, axis=dim), axis, backward)
        block = jnp.concatenate([low, block, high], axis=dim)
    return block


def mirror(stacked):
    groups, rows_here, col_count = stacked.shape
    piece_count = lax.axis_size(("col", "sub"))
    band_count = lax.axis_size("row")
    piece_len = rows_here // piece_count
    split_rows = stacked.reshape(groups, piece_count, piece_len, col_count)
    arrived = lax.all_to_all(split_rows, ("col", "sub"), split_axis=1, concat_axis=1, tiled=True)
    turned = jnp.swapaxes(arrived.reshape(groups, rows_here, col_count), 1, 2).reshape(
        groups, band_count, piece_len, rows_here
    )
    landed = lax.all_to_all(turned, "row", split_axis=1, concat_axis=1, tiled=True)
    spread = landed.reshape(groups, band_count, piece_len, piece_count, piece_len)
    placed = jnp.transpose(spread, (0, 3, 2, 1, 4))
    return placed.reshape(groups, rows_here, col_count)


def banded_body(packed, h_real, h_imag, h_cols):
    packed_here = packed.reshape(packed.shape[1], packed.shape[2])
    rows_here, col_count = packed_here.shape
    band_index = lax.axis_index("row")
    piece_index = lax.axis_index(("col", "sub"))
    piece_len = rows_here // lax.axis_size(("col", "sub"))
    flipped = mirror(packed_here[None])[0]
    row_ids = band_index * rows_here + jnp.arange(rows_here, dtype=jnp.int32)[:, None]
    col_local = jnp.arange(col_count, dtype=jnp.int32)[None, :]
    col_ids = col_local // piece_len * rows_here + piece_index * piece_len + col_local % piece_len
    upper_mask = row_ids <= col_ids
    real_part = jnp.where(upper_mask, packed_here, flipped)
    imag_part = jnp.where(
        row_ids > col_ids,
        packed_here,
        jnp.where(row_ids < col_ids, -flipped, jnp.zeros_like(flipped)),
    )
    current = jnp.stack([real_part, imag_part])
    summed = current.astype(jnp.float32)
    combined = jnp.stack([jnp.stack([h_imag, h_real], 2), jnp.stack([-h_real, h_imag], 2)])
    local_blocks = h_real.shape[0]
    block_len = h_real.shape[2]
    block_total = lax.axis_size("row") * local_blocks
    block_ids = band_index * local_blocks + jnp.arange(local_blocks, dtype=jnp.int32)[:, None]
    offsets = (h_cols - block_ids + 2) % block_total - 2
    starts = (
        (jnp.arange(local_blocks, dtype=jnp.int32)[:, None] + offsets + 2) * block_len
    ).reshape(-1)
    for term_index in range(1, TERMS + 1):
        padded = extended(current, (("row", 1),), 2 * block_len)
        sliced = jnp.stack(
            [
                lax.dynamic_slice_in_dim(padded, starts[k], block_len, 1)
                for k in range(starts.shape[0])
            ]
        )
        gathered = sliced.reshape(local_blocks, 4, 2, block_len, col_count)
        product = jnp.einsum(
            "obsgij,bsgjc->obic", combined, gathered, preferred_element_type=jnp.float32
        )
        generator = product.reshape(2, rows_here, col_count).astype(jnp.bfloat16)
        mirror_part = mirror(generator).astype(jnp.float32)
        own_part = generator.astype(jnp.float32)
        update = (
            step_size
            / term_index
            * jnp.stack([own_part[0] + mirror_part[0], own_part[1] - mirror_part[1]])
        )
        summed = summed + update
        current = update.astype(jnp.bfloat16)
    result = jnp.where(upper_mask, summed[0], summed[1])
    return result[None]


VMEM_BYTES = 56 * 2**20
NEAR_VMEM = 8 * 2**20
POWERS_VMEM = 20 * 2**20
MAIN_VMEM = 22 * 2**20
OWN_VMEM = 14 * 2**20
F32 = jnp.float32
BF16 = jnp.bfloat16


def exchange(block, axes, offset):
    count = lax.axis_size(axes)
    return lax.ppermute(block, axes, [(i, i ^ offset) for i in range(count)])


def block_product(dims, facts, h_refs, at, take):
    bands, rows, cols, piece, local, count, block, per = dims
    starts = []
    for side in (0, 1):
        for a in range(per):
            s = lax.bitwise_xor(facts[3], side) * per + a
            column = facts[4 + at * count + s]
            slot = lax.bitwise_xor(column // local, facts[0])
            starts.append(pl.multiple_of((slot * local + column % local) * block, block))
    right = jnp.concatenate([take(pl.ds(start, block)) for start in starts], axis=0)
    return jnp.dot(
        jnp.concatenate([ref[at] for ref in h_refs], axis=1), right, preferred_element_type=F32
    )


def apply_a(dims, facts, h_refs, at, take, width):
    block = dims[6]
    got = block_product(dims, facts, h_refs, at, take)
    real = got[:block, :width] + got[block:, width:]
    imag = got[:block, width:] - got[block:, :width]
    return 0.5 * jnp.concatenate([real, imag], axis=1)


def place_side(dims, facts, side, mine_ref, part_ref, h_ref):
    bands, rows, cols, piece, local, count, block, per = dims
    core = lax.bitwise_xor(facts[3], side)
    wide = per * block
    for b in range(local):
        h_ref[b] = mine_ref[b, :, pl.ds(pl.multiple_of(core * wide, wide), wide)]
    for n in range(part_ref.shape[0]):
        flat = (lax.bitwise_xor(facts[2], n) * 2 + core) * per
        below = pl.ds(pl.multiple_of((1 - flat // (local * count)) * block, block), block)
        b = flat // count % local
        for k in range(1, bands):
            for at in range(per):
                h_ref[k * local + b, below, at * block : (at + 1) * block] = part_ref[
                    n, k - 1, at * block : (at + 1) * block, :
                ]


def near_kernel(dims, facts, mine_ref, near_ref, h_ref, sel_ref):
    bands, rows, cols, piece, local, count, block, per = dims
    place_side(dims, facts, 0, mine_ref, near_ref, h_ref)
    row_iota = lax.broadcasted_iota(jnp.int32, (rows, cols), 0)
    col_iota = lax.broadcasted_iota(jnp.int32, (rows, cols), 1)
    for k in range(bands):
        hit = (col_iota // piece == k) & (row_iota == facts[1] * piece + col_iota % piece)
        sel_ref[k * rows : (k + 1) * rows, :] = jnp.where(hit, 1.0, 0.0).astype(BF16)


def powers_kernel(dims, facts, mine_ref, far_ref, near_h, sel, far_h, c_ref, c1_ref, c2_ref, csum):
    bands, rows, cols, piece, local, count, block, per = dims
    place_side(dims, facts, 1, mine_ref, far_ref, far_h)
    h_refs = (near_h, far_h)

    def put_d(span, m, value):
        low = value.astype(BF16)
        c_ref[span, m * cols : (m + 1) * cols] = low[:, :cols]
        c_ref[span, (m + 3) * cols : (m + 4) * cols] = low[:, cols:]

    for at in range(bands * local):
        span = slice(at * block, (at + 1) * block)
        got = block_product(dims, facts, h_refs, at, lambda where: sel[where, :])
        c1 = 0.5 * jnp.concatenate([got[:block], -got[block:]], axis=1)
        c1_ref[span, :] = c1.astype(BF16)
        csum[span, :] = c1
        put_d(span, 2, 0.5 * c1)
    for at in range(bands * local):
        span = slice(at * block, (at + 1) * block)
        c2 = apply_a(dims, facts, h_refs, at, lambda where: c1_ref[where, :], cols)
        c2_ref[span, :] = c2.astype(BF16)
        both = csum[span, :] + 0.5 * c2
        csum[span, :] = both
        put_d(span, 1, both)
    for at in range(bands * local):
        span = slice(at * block, (at + 1) * block)
        c3 = apply_a(dims, facts, h_refs, at, lambda where: c2_ref[where, :], cols)
        put_d(span, 0, csum[span, :] + c3 * (1.0 / 6.0))


def swap_groups(value, r, piece):
    size = value.shape[1]
    groups = size // piece
    bit = 1
    while bit < groups:
        moved = jnp.concatenate(
            [value[:, (g ^ bit) * piece : (g ^ bit) * piece + piece] for g in range(groups)], axis=1
        )
        value = jnp.where(lax.bitwise_and(r, bit) != 0, moved, value)
        bit *= 2
    return value


def products(dims, facts, wanted, c_ref, n_ref, v1_ref, v2_ref, left, slab, outs):
    bands, rows, cols, piece, local, count, block, per = dims
    r, q = facts[0], facts[1]
    nt = (((1,), (1,)), ((), ()))
    size = len(wanted) * piece
    spans = [
        [pl.ds(pl.multiple_of(k * rows + p * piece, piece), piece) for p in wanted] for k in range(bands)
    ]
    i_own = lax.broadcasted_iota(jnp.int32, (piece, rows), 1)
    j_own = lax.broadcasted_iota(jnp.int32, (piece, rows), 0)
    upper = jnp.concatenate([i_own <= p * piece + j_own for p in wanted], axis=0)
    mine = lax.broadcasted_iota(jnp.int32, (size, rows), 1) // piece == q

    def against(which, slots):
        right = jnp.concatenate(
            [
                jnp.concatenate([ref[span, :] for ref in (c_ref, n_ref, v1_ref, v2_ref)], axis=1)
                for k in slots
                for span in spans[k]
            ],
            axis=0,
        )
        return lax.dot_general(right, left[which], nt, preferred_element_type=F32)

    for k in range(0, bands, 2):
        if k == 0:
            next_side = (lax.bitwise_xor(r, 1) < r).astype(jnp.int32)
            got = [jnp.where(upper, against(0, (0,)), against(1, (0,))), against(next_side, (1,))]
        else:
            side = against((lax.bitwise_xor(r, k) < r).astype(jnp.int32), (k, k + 1))
            got = [side[:size], side[size:]]
        for n in (0, 1):
            thin = jnp.concatenate([slab[span, :] for span in spans[k + n]], axis=0)
            real = jnp.concatenate([thin[:, :piece]] * (rows // piece), axis=1)
            imag = jnp.concatenate([-thin[:, piece:]] * (rows // piece), axis=1)
            above = upper if k + n == 0 else lax.bitwise_xor(r, k + n) > r
            outs[k + n] = got[n] + jnp.where(mine, jnp.where(above, real, imag), 0.0)

    def target(n):
        return jnp.concatenate(
            [outs[lax.bitwise_xor(r, b), n * piece : (n + 1) * piece, :] for b in range(bands)], axis=0
        ).T

    return target


def main_kernel(dims, facts, *refs):
    bands, rows, cols, piece, local, count, block, per = dims
    f_refs = refs[:bands]
    near_h, far_h, c_ref, keep_ref, send_ref, n_ref, v1_ref, v2_ref, left, slab, tops, outs = refs[bands:]
    h_refs = (near_h, far_h)
    r, q = facts[0], facts[1]
    row_iota = lax.broadcasted_iota(jnp.int32, (rows, cols), 0)
    col_iota = lax.broadcasted_iota(jnp.int32, (rows, cols), 1)
    col_abs = lax.bitwise_xor(col_iota // piece, r) * rows + q * piece + col_iota % piece
    for k in range(bands):
        here = swap_groups(f_refs[-k % bands][...].astype(F32), r, piece)
        row_abs = lax.bitwise_xor(r, k) * rows + row_iota
        real = jnp.where(row_abs < col_abs, here, jnp.where(row_abs == col_abs, 0.5 * here, 0.0))
        imag = jnp.where(row_abs > col_abs, here, 0.0)
        n_ref[k * rows : (k + 1) * rows, :] = jnp.concatenate([real, imag], axis=1).astype(BF16)

    def thin(value):
        return jnp.concatenate([value[:, :piece], value[:, cols : cols + piece]], axis=1)

    for at in range(bands * local):
        span = slice(at * block, (at + 1) * block)
        v1 = apply_a(dims, facts, h_refs, at, lambda where: n_ref[where, :], cols)
        v1_ref[span, :] = v1.astype(BF16)
        slab[span, :] = thin(v1)
        if at < local:
            tops[span, :] = v1
    for at in range(bands * local):
        span = slice(at * block, (at + 1) * block)
        v2 = apply_a(dims, facts, h_refs, at, lambda where: v1_ref[where, :], cols)
        v2_ref[span, :] = v2.astype(BF16)
        slab[span, :] += 0.5 * thin(v2)
        if at < local:
            tops[span, :] += 0.5 * v2
    for at in range(bands * local):
        span = slice(at * block, (at + 1) * block)
        if at < local:
            v3 = apply_a(dims, facts, h_refs, at, lambda where: v2_ref[where, :], cols)
            tops[span, :] += v3 * (1.0 / 6.0)
            slab[span, :] += thin(v3) * (1.0 / 6.0)
        else:
            v3 = apply_a(
                dims,
                facts,
                h_refs,
                at,
                lambda where: jnp.concatenate(
                    [v2_ref[where, 0:piece], v2_ref[where, cols : cols + piece]],
                    axis=1,
                ),
                piece,
            )
            slab[span, :] += v3 * (1.0 / 6.0)
    own = slice(0, rows)
    three = 3 * cols
    for m, t_ref in enumerate((n_ref, v1_ref, v2_ref)):
        tr, ti = t_ref[own, :cols], t_ref[own, cols:]
        cr = c_ref[own, m * cols : (m + 1) * cols]
        ci = c_ref[own, three + m * cols : three + (m + 1) * cols]
        for which, (first, second, third, fourth) in enumerate(((tr, ti, cr, ci), (ti, -tr, ci, -cr))):
            left[which, :, m * cols : (m + 1) * cols] = first
            left[which, :, three + m * cols : three + (m + 1) * cols] = second
            left[which, :, 2 * three + 2 * m * cols : 2 * three + (2 * m + 1) * cols] = third
            left[which, :, 2 * three + (2 * m + 1) * cols : 2 * three + (2 * m + 2) * cols] = fourth
    far = lax.bitwise_xor(q, 2)
    wanted = (lax.bitwise_xor(far, 1), lax.bitwise_xor(q, 1), far)
    target = products(dims, facts, wanted, c_ref, n_ref, v1_ref, v2_ref, left, slab, outs)
    send_ref[0] = target(0)
    send_ref[1] = target(1)
    keep_ref[...] = target(2)


def own_kernel(dims, facts, c_ref, n_ref, v1_ref, v2_ref, left, slab, tops, own_ref, outs):
    bands, rows, cols, piece, local, count, block, per = dims
    r, q = facts[0], facts[1]
    target = products(dims, facts, (q,), c_ref, n_ref, v1_ref, v2_ref, left, slab, outs)
    col_iota = lax.broadcasted_iota(jnp.int32, (rows, cols), 1)
    col_abs = col_iota // piece * rows + q * piece + col_iota % piece
    row_abs = r * rows + lax.broadcasted_iota(jnp.int32, (rows, cols), 0)
    real = swap_groups(tops[:, :cols], r, piece)
    imag = swap_groups(tops[:, cols:], r, piece)
    own_ref[...] = target(0) + jnp.where(row_abs <= col_abs, real, imag)


def gathered_body(packed, h_real, h_imag, h_cols):
    here = packed.reshape(packed.shape[1], packed.shape[2])
    rows, cols = here.shape
    bands = lax.axis_size("row")
    piece = rows // lax.axis_size(("col", "sub"))
    local, count, block = h_real.shape[0], h_real.shape[1], h_real.shape[2]
    order = bands * rows
    r = lax.axis_index("row")
    q = lax.axis_index(("col", "sub"))
    me_plane = lax.axis_index(("runs", "col"))
    me_core = lax.axis_index("sub")
    shares = lax.axis_size(("runs", "col", "sub"))
    per = 2 * local * count // shares
    dims = (bands, rows, cols, piece, local, count, block, per)

    smem = pl.BlockSpec(memory_space=pltpu.SMEM)
    vmem = pl.BlockSpec(memory_space=pltpu.VMEM)
    flat_real, flat_imag = [h.reshape(local * count, block, block) for h in (h_real, h_imag)]

    def pick(first, second, at):
        return jnp.where(
            lax.axis_index("runs") == 0,
            lax.dynamic_slice_in_dim(first, at * per, per, 0),
            lax.dynamic_slice_in_dim(second, at * per, per, 0),
        ).reshape(per * block, block)

    size = per * block
    col_rows = jnp.pad(h_cols.astype(BF16), ((0, 16 - local), (0, block - count)))
    message = jnp.concatenate([pick(flat_real, flat_imag, q), col_rows], axis=0)
    diagonal = pick(flat_imag, flat_real, lax.bitwise_xor(q, 2))
    mine = jnp.concatenate(
        [h.transpose(0, 2, 1, 3).reshape(local, block, count * block) for h in (h_imag, h_real)], axis=1
    )
    arrived = [exchange(message, "row", k) for k in range(1, bands)]
    all_cols = [a[size : size + local, :count].astype(jnp.int32).reshape(-1) for a in [message] + arrived]
    facts = jnp.concatenate([jnp.stack([r, q, me_plane, me_core]).astype(jnp.int32)] + all_cols)
    theirs = lax.optimization_barrier(jnp.stack([a[:size] for a in arrived]))
    across_plane = jnp.concatenate([exchange(diagonal, "row", 1)[None], exchange(theirs[1:], ("runs", "col"), 3)], axis=0)
    near = jnp.stack([theirs] + [exchange(theirs, ("runs", "col"), k) for k in (1, 2)] + [across_plane])
    rest = [exchange(here, "row", k) for k in range(bands - 1, 0, -1)]
    far = exchange(near, "sub", 1)

    step = 2 * order * 2 * count * block * 2 * cols
    half_shape = jax.ShapeDtypeStruct((bands * local, 2 * block, per * block), BF16)
    near_h, sel = pl.pallas_call(
        functools.partial(near_kernel, dims),
        out_shape=(half_shape, jax.ShapeDtypeStruct((order, cols), BF16)),
        in_specs=[smem] + [vmem] * 2,
        out_specs=(vmem, vmem),
        compiler_params=pltpu.CompilerParams(vmem_limit_bytes=NEAR_VMEM),
        cost_estimate=pl.CostEstimate(flops=0, bytes_accessed=2**20, transcendentals=0),
        name="near",
    )(facts, mine, near)
    far_h, c_side = pl.pallas_call(
        functools.partial(powers_kernel, dims),
        out_shape=(half_shape, jax.ShapeDtypeStruct((order, 6 * cols), BF16)),
        in_specs=[smem] + [vmem] * 4,
        out_specs=(vmem, vmem),
        scratch_shapes=[
            pltpu.VMEM((order, 2 * cols), BF16),
            pltpu.VMEM((order, 2 * cols), BF16),
            pltpu.VMEM((order, 2 * cols), F32),
        ],
        compiler_params=pltpu.CompilerParams(vmem_limit_bytes=POWERS_VMEM),
        cost_estimate=pl.CostEstimate(flops=5 * step // 2, bytes_accessed=2**20, transcendentals=0),
        name="powers",
    )(facts, mine, far, near_h, sel)
    block_shape = jax.ShapeDtypeStruct((rows, cols), F32)
    v_shape = jax.ShapeDtypeStruct((order, 2 * cols), BF16)
    keep, send, *state = pl.pallas_call(
        functools.partial(main_kernel, dims),
        out_shape=(
            block_shape,
            jax.ShapeDtypeStruct((2, rows, cols), F32),
            v_shape,
            v_shape,
            v_shape,
            jax.ShapeDtypeStruct((2, rows, 12 * cols), BF16),
            jax.ShapeDtypeStruct((order, 2 * piece), F32),
            jax.ShapeDtypeStruct((rows, 2 * cols), F32),
        ),
        in_specs=[smem] + [vmem] * (bands + 3),
        out_specs=(vmem,) * 8,
        scratch_shapes=[pltpu.VMEM((bands, 3 * piece, rows), F32)],
        compiler_params=pltpu.CompilerParams(vmem_limit_bytes=MAIN_VMEM),
        cost_estimate=pl.CostEstimate(flops=4 * step, bytes_accessed=2**20, transcendentals=0),
        name="main",
    )(facts, here, *rest, near_h, far_h, c_side)
    swapped = exchange(send, "sub", 1)
    across = exchange((keep + swapped[0]).astype(BF16), "col", 1)
    own = pl.pallas_call(
        functools.partial(own_kernel, dims),
        out_shape=block_shape,
        in_specs=[smem] + [vmem] * 7,
        out_specs=vmem,
        scratch_shapes=[pltpu.VMEM((bands, piece, rows), F32)],
        compiler_params=pltpu.CompilerParams(vmem_limit_bytes=OWN_VMEM),
        cost_estimate=pl.CostEstimate(flops=step, bytes_accessed=2**20, transcendentals=0),
        name="own",
    )(facts, c_side, *state)
    total = here.astype(F32) + own + swapped[1] + across.astype(F32)
    return total[None]


def can_gather(mesh, local_packed, local_h):
    bands = mesh.shape["row"]
    rows, cols = local_packed[1], local_packed[2]
    local, count, block = local_h[0], local_h[1], local_h[2]
    shares = mesh.shape["runs"] * mesh.shape["col"] * mesh.shape["sub"]
    return (
        bands & (bands - 1) == 0
        and bands > 2
        and mesh.shape["runs"] == mesh.shape["col"] == mesh.shape["sub"] == 2
        and rows == cols == local * block
        and (2 * local * count) % shares == 0
        and local <= 16
        and count * shares == 4 * local * count
        and count <= block
        and 80 * bands * rows * bands * rows // 2 <= VMEM_BYTES
    )


def body(mesh, packed, h_real, h_imag, h_cols):
    if can_gather(mesh, packed.shape, h_real.shape):
        return gathered_body(packed, h_real, h_imag, h_cols)
    return banded_body(packed, h_real, h_imag, h_cols)


def solution(mesh):
    in_specs = (
        P(("col", "sub"), ("runs", "row"), None),
        P("row", None, None, None),
        P("row", None, None, None),
        P("row", None),
    )
    out_specs = P(("col", "sub"), ("runs", "row"), None)
    return jax.shard_map(
        functools.partial(body, mesh), mesh=mesh, in_specs=in_specs, out_specs=out_specs, check_vma=False
    )
```

```python
import functools

import jax
import jax.numpy as jnp
from jax import lax
from jax.experimental import pallas as pl
from jax.experimental.pallas import tpu as pltpu
from jax.sharding import PartitionSpec as P

TERMS = 3


step_size = 0.5


def extended(block, sides, width):
    for axis, dim in sides:
        count = lax.axis_size(axis)
        forward = [(i, i + 1) for i in range(count - 1)]
        forward.append((count - 1, 0))
        backward = [(target, source) for source, target in forward]
        low = lax.ppermute(
            lax.slice_in_dim(block, block.shape[dim] - width, None, axis=dim), axis, forward
        )
        high = lax.ppermute(lax.slice_in_dim(block, 0, width, axis=dim), axis, backward)
        block = jnp.concatenate([low, block, high], axis=dim)
    return block


def mirror(stacked):
    groups, rows_here, col_count = stacked.shape
    piece_count = lax.axis_size(("col", "sub"))
    band_count = lax.axis_size("row")
    piece_len = rows_here // piece_count
    split_rows = stacked.reshape(groups, piece_count, piece_len, col_count)
    arrived = lax.all_to_all(split_rows, ("col", "sub"), split_axis=1, concat_axis=1, tiled=True)
    turned = jnp.swapaxes(arrived.reshape(groups, rows_here, col_count), 1, 2).reshape(
        groups, band_count, piece_len, rows_here
    )
    landed = lax.all_to_all(turned, "row", split_axis=1, concat_axis=1, tiled=True)
    spread = landed.reshape(groups, band_count, piece_len, piece_count, piece_len)
    placed = jnp.transpose(spread, (0, 3, 2, 1, 4))
    return placed.reshape(groups, rows_here, col_count)


def banded_body(packed, h_real, h_imag, h_cols):
    packed_here = packed.reshape(packed.shape[1], packed.shape[2])
    rows_here, col_count = packed_here.shape
    band_index = lax.axis_index("row")
    piece_index = lax.axis_index(("col", "sub"))
    piece_len = rows_here // lax.axis_size(("col", "sub"))
    flipped = mirror(packed_here[None])[0]
    row_ids = band_index * rows_here + jnp.arange(rows_here, dtype=jnp.int32)[:, None]
    col_local = jnp.arange(col_count, dtype=jnp.int32)[None, :]
    col_ids = col_local // piece_len * rows_here + piece_index * piece_len + col_local % piece_len
    upper_mask = row_ids <= col_ids
    real_part = jnp.where(upper_mask, packed_here, flipped)
    imag_part = jnp.where(
        row_ids > col_ids,
        packed_here,
        jnp.where(row_ids < col_ids, -flipped, jnp.zeros_like(flipped)),
    )
    current = jnp.stack([real_part, imag_part])
    summed = current.astype(jnp.float32)
    combined = jnp.stack([jnp.stack([h_imag, h_real], 2), jnp.stack([-h_real, h_imag], 2)])
    local_blocks = h_real.shape[0]
    block_len = h_real.shape[2]
    block_total = lax.axis_size("row") * local_blocks
    block_ids = band_index * local_blocks + jnp.arange(local_blocks, dtype=jnp.int32)[:, None]
    offsets = (h_cols - block_ids + 2) % block_total - 2
    starts = (
        (jnp.arange(local_blocks, dtype=jnp.int32)[:, None] + offsets + 2) * block_len
    ).reshape(-1)
    for term_index in range(1, TERMS + 1):
        padded = extended(current, (("row", 1),), 2 * block_len)
        sliced = jnp.stack(
            [
                lax.dynamic_slice_in_dim(padded, starts[k], block_len, 1)
                for k in range(starts.shape[0])
            ]
        )
        gathered = sliced.reshape(local_blocks, 4, 2, block_len, col_count)
        product = jnp.einsum(
            "obsgij,bsgjc->obic", combined, gathered, preferred_element_type=jnp.float32
        )
        generator = product.reshape(2, rows_here, col_count).astype(jnp.bfloat16)
        mirror_part = mirror(generator).astype(jnp.float32)
        own_part = generator.astype(jnp.float32)
        update = (
            step_size
            / term_index
            * jnp.stack([own_part[0] + mirror_part[0], own_part[1] - mirror_part[1]])
        )
        summed = summed + update
        current = update.astype(jnp.bfloat16)
    result = jnp.where(upper_mask, summed[0], summed[1])
    return result[None]


VMEM_BYTES = 56 * 2**20
NEAR_VMEM = 8 * 2**20
POWERS_VMEM = 20 * 2**20
MAIN_VMEM = 22 * 2**20
OWN_VMEM = 14 * 2**20
F32 = jnp.float32
BF16 = jnp.bfloat16


def exchange(block, axes, offset):
    count = lax.axis_size(axes)
    return lax.ppermute(block, axes, [(i, i ^ offset) for i in range(count)])


def block_product(dims, facts, h_refs, at, take):
    bands, rows, cols, piece, local, count, block, per = dims
    starts = []
    for side in (0, 1):
        for a in range(per):
            s = lax.bitwise_xor(facts[3], side) * per + a
            column = facts[4 + at * count + s]
            slot = lax.bitwise_xor(column // local, facts[0])
            starts.append(pl.multiple_of((slot * local + column % local) * block, block))
    right = jnp.concatenate([take(pl.ds(start, block)) for start in starts], axis=0)
    return jnp.dot(
        jnp.concatenate([ref[at] for ref in h_refs], axis=1), right, preferred_element_type=F32
    )


def apply_a(dims, facts, h_refs, at, take, width):
    block = dims[6]
    got = block_product(dims, facts, h_refs, at, take)
    real = got[:block, :width] + got[block:, width:]
    imag = got[:block, width:] - got[block:, :width]
    return 0.5 * jnp.concatenate([real, imag], axis=1)


def place_side(dims, facts, side, mine_ref, part_ref, h_ref):
    bands, rows, cols, piece, local, count, block, per = dims
    core = lax.bitwise_xor(facts[3], side)
    wide = per * block
    for b in range(local):
        h_ref[b] = mine_ref[b, :, pl.ds(pl.multiple_of(core * wide, wide), wide)]
    for n in range(part_ref.shape[0]):
        flat = (lax.bitwise_xor(facts[2], n) * 2 + core) * per
        below = pl.ds(pl.multiple_of((1 - flat // (local * count)) * block, block), block)
        b = flat // count % local
        for k in range(1, bands):
            for at in range(per):
                h_ref[k * local + b, below, at * block : (at + 1) * block] = part_ref[
                    n, k - 1, at * block : (at + 1) * block, :
                ]


def near_kernel(dims, facts, mine_ref, near_ref, h_ref, sel_ref):
    bands, rows, cols, piece, local, count, block, per = dims
    place_side(dims, facts, 0, mine_ref, near_ref, h_ref)
    row_iota = lax.broadcasted_iota(jnp.int32, (rows, cols), 0)
    col_iota = lax.broadcasted_iota(jnp.int32, (rows, cols), 1)
    for k in range(bands):
        hit = (col_iota // piece == k) & (row_iota == facts[1] * piece + col_iota % piece)
        sel_ref[k * rows : (k + 1) * rows, :] = jnp.where(hit, 1.0, 0.0).astype(BF16)


def powers_kernel(dims, facts, mine_ref, far_ref, near_h, sel, far_h, c_ref, c1_ref, c2_ref, csum):
    bands, rows, cols, piece, local, count, block, per = dims
    place_side(dims, facts, 1, mine_ref, far_ref, far_h)
    h_refs = (near_h, far_h)

    def put_d(span, m, value):
        low = value.astype(BF16)
        c_ref[span, m * cols : (m + 1) * cols] = low[:, :cols]
        c_ref[span, (m + 3) * cols : (m + 4) * cols] = low[:, cols:]

    for at in range(bands * local):
        span = slice(at * block, (at + 1) * block)
        got = block_product(dims, facts, h_refs, at, lambda where: sel[where, :])
        c1 = 0.5 * jnp.concatenate([got[:block], -got[block:]], axis=1)
        c1_ref[span, :] = c1.astype(BF16)
        csum[span, :] = c1
        put_d(span, 2, 0.5 * c1)
    for at in range(bands * local):
        span = slice(at * block, (at + 1) * block)
        c2 = apply_a(dims, facts, h_refs, at, lambda where: c1_ref[where, :], cols)
        c2_ref[span, :] = c2.astype(BF16)
        both = csum[span, :] + 0.5 * c2
        csum[span, :] = both
        put_d(span, 1, both)
    for at in range(bands * local):
        span = slice(at * block, (at + 1) * block)
        c3 = apply_a(dims, facts, h_refs, at, lambda where: c2_ref[where, :], cols)
        put_d(span, 0, csum[span, :] + c3 * (1.0 / 6.0))


def swap_groups(value, r, piece):
    size = value.shape[1]
    groups = size // piece
    bit = 1
    while bit < groups:
        moved = jnp.concatenate(
            [value[:, (g ^ bit) * piece : (g ^ bit) * piece + piece] for g in range(groups)], axis=1
        )
        value = jnp.where(lax.bitwise_and(r, bit) != 0, moved, value)
        bit *= 2
    return value


def products(dims, facts, wanted, c_ref, n_ref, v1_ref, v2_ref, left, slab, outs):
    bands, rows, cols, piece, local, count, block, per = dims
    r, q = facts[0], facts[1]
    nt = (((1,), (1,)), ((), ()))
    size = len(wanted) * piece
    spans = [
        [pl.ds(pl.multiple_of(k * rows + p * piece, piece), piece) for p in wanted] for k in range(bands)
    ]
    i_own = lax.broadcasted_iota(jnp.int32, (piece, rows), 1)
    j_own = lax.broadcasted_iota(jnp.int32, (piece, rows), 0)
    upper = jnp.concatenate([i_own <= p * piece + j_own for p in wanted], axis=0)
    mine = lax.broadcasted_iota(jnp.int32, (size, rows), 1) // piece == q

    def against(which, slots):
        right = jnp.concatenate(
            [
                jnp.concatenate([ref[span, :] for ref in (c_ref, n_ref, v1_ref, v2_ref)], axis=1)
                for k in slots
                for span in spans[k]
            ],
            axis=0,
        )
        return lax.dot_general(right, left[which], nt, preferred_element_type=F32)

    for k in range(0, bands, 2):
        if k == 0:
            next_side = (lax.bitwise_xor(r, 1) < r).astype(jnp.int32)
            got = [jnp.where(upper, against(0, (0,)), against(1, (0,))), against(next_side, (1,))]
        else:
            side = against((lax.bitwise_xor(r, k) < r).astype(jnp.int32), (k, k + 1))
            got = [side[:size], side[size:]]
        for n in (0, 1):
            thin = jnp.concatenate([slab[span, :] for span in spans[k + n]], axis=0)
            real = jnp.concatenate([thin[:, :piece]] * (rows // piece), axis=1)
            imag = jnp.concatenate([-thin[:, piece:]] * (rows // piece), axis=1)
            above = upper if k + n == 0 else lax.bitwise_xor(r, k + n) > r
            outs[k + n] = got[n] + jnp.where(mine, jnp.where(above, real, imag), 0.0)

    def target(n):
        return jnp.concatenate(
            [outs[lax.bitwise_xor(r, b), n * piece : (n + 1) * piece, :] for b in range(bands)], axis=0
        ).T

    return target


def main_kernel(dims, facts, *refs):
    bands, rows, cols, piece, local, count, block, per = dims
    f_refs = refs[:bands]
    near_h, far_h, c_ref, keep_ref, send_ref, n_ref, v1_ref, v2_ref, left, slab, tops, outs = refs[bands:]
    h_refs = (near_h, far_h)
    r, q = facts[0], facts[1]
    row_iota = lax.broadcasted_iota(jnp.int32, (rows, cols), 0)
    col_iota = lax.broadcasted_iota(jnp.int32, (rows, cols), 1)
    col_abs = lax.bitwise_xor(col_iota // piece, r) * rows + q * piece + col_iota % piece
    for k in range(bands):
        here = swap_groups(f_refs[-k % bands][...].astype(F32), r, piece)
        row_abs = lax.bitwise_xor(r, k) * rows + row_iota
        real = jnp.where(row_abs < col_abs, here, jnp.where(row_abs == col_abs, 0.5 * here, 0.0))
        imag = jnp.where(row_abs > col_abs, here, 0.0)
        n_ref[k * rows : (k + 1) * rows, :] = jnp.concatenate([real, imag], axis=1).astype(BF16)

    def thin(value):
        return jnp.concatenate([value[:, :piece], value[:, cols : cols + piece]], axis=1)

    for at in range(bands * local):
        span = slice(at * block, (at + 1) * block)
        v1 = apply_a(dims, facts, h_refs, at, lambda where: n_ref[where, :], cols)
        v1_ref[span, :] = v1.astype(BF16)
        slab[span, :] = thin(v1)
        if at < local:
            tops[span, :] = v1
    for at in range(bands * local):
        span = slice(at * block, (at + 1) * block)
        v2 = apply_a(dims, facts, h_refs, at, lambda where: v1_ref[where, :], cols)
        v2_ref[span, :] = v2.astype(BF16)
        slab[span, :] += 0.5 * thin(v2)
        if at < local:
            tops[span, :] += 0.5 * v2
    for at in range(bands * local):
        span = slice(at * block, (at + 1) * block)
        v3 = apply_a(
            dims,
            facts,
            h_refs,
            at,
            lambda where: jnp.concatenate([v2_ref[where, 0:piece], v2_ref[where, cols : cols + piece]], axis=1),
            piece,
        )
        slab[span, :] += v3 * (1.0 / 6.0)
    own = slice(0, rows)
    three = 3 * cols
    for m, t_ref in enumerate((n_ref, v1_ref, v2_ref)):
        tr, ti = t_ref[own, :cols], t_ref[own, cols:]
        cr = c_ref[own, m * cols : (m + 1) * cols]
        ci = c_ref[own, three + m * cols : three + (m + 1) * cols]
        for which, (first, second, third, fourth) in enumerate(((tr, ti, cr, ci), (ti, -tr, ci, -cr))):
            left[which, :, m * cols : (m + 1) * cols] = first
            left[which, :, three + m * cols : three + (m + 1) * cols] = second
            left[which, :, 2 * three + 2 * m * cols : 2 * three + (2 * m + 1) * cols] = third
            left[which, :, 2 * three + (2 * m + 1) * cols : 2 * three + (2 * m + 2) * cols] = fourth
    far = lax.bitwise_xor(q, 2)
    wanted = (lax.bitwise_xor(far, 1), lax.bitwise_xor(q, 1), far)
    target = products(dims, facts, wanted, c_ref, n_ref, v1_ref, v2_ref, left, slab, outs)
    send_ref[0] = target(0).astype(BF16)
    send_ref[1] = target(1).astype(BF16)
    keep_ref[...] = target(2)


def own_kernel(dims, facts, near_h, far_h, c_ref, n_ref, v1_ref, v2_ref, left, slab, tops, own_ref, outs):
    bands, rows, cols, piece, local, count, block, per = dims
    r, q = facts[0], facts[1]
    target = products(dims, facts, (q,), c_ref, n_ref, v1_ref, v2_ref, left, slab, outs)
    col_iota = lax.broadcasted_iota(jnp.int32, (rows, cols), 1)
    col_abs = col_iota // piece * rows + q * piece + col_iota % piece
    row_abs = r * rows + lax.broadcasted_iota(jnp.int32, (rows, cols), 0)
    v3 = jnp.concatenate(
        [apply_a(dims, facts, (near_h, far_h), at, lambda where: v2_ref[where, :], cols) for at in range(local)],
        axis=0,
    )
    direct = tops[...] + v3 * (1.0 / 6.0)
    real = swap_groups(direct[:, :cols], r, piece)
    imag = swap_groups(direct[:, cols:], r, piece)
    own_ref[...] = target(0) + jnp.where(row_abs <= col_abs, real, imag)


def gathered_body(packed, h_real, h_imag, h_cols):
    here = packed.reshape(packed.shape[1], packed.shape[2])
    rows, cols = here.shape
    bands = lax.axis_size("row")
    piece = rows // lax.axis_size(("col", "sub"))
    local, count, block = h_real.shape[0], h_real.shape[1], h_real.shape[2]
    order = bands * rows
    r = lax.axis_index("row")
    q = lax.axis_index(("col", "sub"))
    me_plane = lax.axis_index(("runs", "col"))
    me_core = lax.axis_index("sub")
    shares = lax.axis_size(("runs", "col", "sub"))
    per = 2 * local * count // shares
    dims = (bands, rows, cols, piece, local, count, block, per)

    smem = pl.BlockSpec(memory_space=pltpu.SMEM)
    vmem = pl.BlockSpec(memory_space=pltpu.VMEM)
    flat_real, flat_imag = [h.reshape(local * count, block, block) for h in (h_real, h_imag)]

    def pick(first, second, at):
        return jnp.where(
            lax.axis_index("runs") == 0,
            lax.dynamic_slice_in_dim(first, at * per, per, 0),
            lax.dynamic_slice_in_dim(second, at * per, per, 0),
        ).reshape(per * block, block)

    size = per * block
    col_rows = jnp.pad(h_cols.astype(BF16), ((0, 16 - local), (0, block - count)))
    message = jnp.concatenate([pick(flat_real, flat_imag, q), col_rows], axis=0)
    diagonal = pick(flat_imag, flat_real, lax.bitwise_xor(q, 2))
    mine = jnp.concatenate(
        [h.transpose(0, 2, 1, 3).reshape(local, block, count * block) for h in (h_imag, h_real)], axis=1
    )
    arrived = [exchange(message, "row", k) for k in range(1, bands)]
    all_cols = [a[size : size + local, :count].astype(jnp.int32).reshape(-1) for a in [message] + arrived]
    facts = jnp.concatenate([jnp.stack([r, q, me_plane, me_core]).astype(jnp.int32)] + all_cols)
    theirs = lax.optimization_barrier(jnp.stack([a[:size] for a in arrived]))
    across_plane = jnp.concatenate([exchange(diagonal, "row", 1)[None], exchange(theirs[1:], ("runs", "col"), 3)], axis=0)
    near = jnp.stack([theirs] + [exchange(theirs, ("runs", "col"), k) for k in (1, 2)] + [across_plane])
    rest = [exchange(here, "row", k) for k in range(bands - 1, 0, -1)]
    far = exchange(near, "sub", 1)

    step = 2 * order * 2 * count * block * 2 * cols
    half_shape = jax.ShapeDtypeStruct((bands * local, 2 * block, per * block), BF16)
    near_h, sel = pl.pallas_call(
        functools.partial(near_kernel, dims),
        out_shape=(half_shape, jax.ShapeDtypeStruct((order, cols), BF16)),
        in_specs=[smem] + [vmem] * 2,
        out_specs=(vmem, vmem),
        compiler_params=pltpu.CompilerParams(vmem_limit_bytes=NEAR_VMEM),
        cost_estimate=pl.CostEstimate(flops=0, bytes_accessed=2**20, transcendentals=0),
        name="near",
    )(facts, mine, near)
    far_h, c_side = pl.pallas_call(
        functools.partial(powers_kernel, dims),
        out_shape=(half_shape, jax.ShapeDtypeStruct((order, 6 * cols), BF16)),
        in_specs=[smem] + [vmem] * 4,
        out_specs=(vmem, vmem),
        scratch_shapes=[
            pltpu.VMEM((order, 2 * cols), BF16),
            pltpu.VMEM((order, 2 * cols), BF16),
            pltpu.VMEM((order, 2 * cols), F32),
        ],
        compiler_params=pltpu.CompilerParams(vmem_limit_bytes=POWERS_VMEM),
        cost_estimate=pl.CostEstimate(flops=5 * step // 2, bytes_accessed=2**20, transcendentals=0),
        name="powers",
    )(facts, mine, far, near_h, sel)
    block_shape = jax.ShapeDtypeStruct((rows, cols), F32)
    v_shape = jax.ShapeDtypeStruct((order, 2 * cols), BF16)
    keep, send, *state = pl.pallas_call(
        functools.partial(main_kernel, dims),
        out_shape=(
            block_shape,
            jax.ShapeDtypeStruct((2, rows, cols), BF16),
            v_shape,
            v_shape,
            v_shape,
            jax.ShapeDtypeStruct((2, rows, 12 * cols), BF16),
            jax.ShapeDtypeStruct((order, 2 * piece), F32),
            jax.ShapeDtypeStruct((rows, 2 * cols), F32),
        ),
        in_specs=[smem] + [vmem] * (bands + 3),
        out_specs=(vmem,) * 8,
        scratch_shapes=[pltpu.VMEM((bands, 3 * piece, rows), F32)],
        compiler_params=pltpu.CompilerParams(vmem_limit_bytes=MAIN_VMEM),
        cost_estimate=pl.CostEstimate(flops=4 * step, bytes_accessed=2**20, transcendentals=0),
        name="main",
    )(facts, here, *rest, near_h, far_h, c_side)
    swapped = exchange(send, "sub", 1)
    across = exchange((keep + swapped[0].astype(F32)).astype(BF16), "col", 1)
    own = pl.pallas_call(
        functools.partial(own_kernel, dims),
        out_shape=block_shape,
        in_specs=[smem] + [vmem] * 9,
        out_specs=vmem,
        scratch_shapes=[pltpu.VMEM((bands, piece, rows), F32)],
        compiler_params=pltpu.CompilerParams(vmem_limit_bytes=OWN_VMEM),
        cost_estimate=pl.CostEstimate(flops=step, bytes_accessed=2**20, transcendentals=0),
        name="own",
    )(facts, near_h, far_h, c_side, *state)
    total = here.astype(F32) + own + swapped[1].astype(F32) + across.astype(F32)
    return total[None]


def can_gather(mesh, local_packed, local_h):
    bands = mesh.shape["row"]
    rows, cols = local_packed[1], local_packed[2]
    local, count, block = local_h[0], local_h[1], local_h[2]
    shares = mesh.shape["runs"] * mesh.shape["col"] * mesh.shape["sub"]
    return (
        bands & (bands - 1) == 0
        and bands > 2
        and mesh.shape["runs"] == mesh.shape["col"] == mesh.shape["sub"] == 2
        and rows == cols == local * block
        and (2 * local * count) % shares == 0
        and local <= 16
        and count * shares == 4 * local * count
        and count <= block
        and 80 * bands * rows * bands * rows // 2 <= VMEM_BYTES
    )


def body(mesh, packed, h_real, h_imag, h_cols):
    if can_gather(mesh, packed.shape, h_real.shape):
        return gathered_body(packed, h_real, h_imag, h_cols)
    return banded_body(packed, h_real, h_imag, h_cols)


def solution(mesh):
    in_specs = (
        P(("col", "sub"), ("runs", "row"), None),
        P("row", None, None, None),
        P("row", None, None, None),
        P("row", None),
    )
    out_specs = P(("col", "sub"), ("runs", "row"), None)
    return jax.shard_map(
        functools.partial(body, mesh), mesh=mesh, in_specs=in_specs, out_specs=out_specs, check_vma=False
    )
```

```python
import functools

import jax
import jax.numpy as jnp
from jax import lax
from jax.experimental import pallas as pl
from jax.experimental.pallas import tpu as pltpu
from jax.sharding import PartitionSpec as P

TERMS = 3


step_size = 0.5


def extended(block, sides, width):
    for axis, dim in sides:
        count = lax.axis_size(axis)
        forward = [(i, i + 1) for i in range(count - 1)]
        forward.append((count - 1, 0))
        backward = [(target, source) for source, target in forward]
        low = lax.ppermute(
            lax.slice_in_dim(block, block.shape[dim] - width, None, axis=dim), axis, forward
        )
        high = lax.ppermute(lax.slice_in_dim(block, 0, width, axis=dim), axis, backward)
        block = jnp.concatenate([low, block, high], axis=dim)
    return block


def mirror(stacked):
    groups, rows_here, col_count = stacked.shape
    piece_count = lax.axis_size(("col", "sub"))
    band_count = lax.axis_size("row")
    piece_len = rows_here // piece_count
    split_rows = stacked.reshape(groups, piece_count, piece_len, col_count)
    arrived = lax.all_to_all(split_rows, ("col", "sub"), split_axis=1, concat_axis=1, tiled=True)
    turned = jnp.swapaxes(arrived.reshape(groups, rows_here, col_count), 1, 2).reshape(
        groups, band_count, piece_len, rows_here
    )
    landed = lax.all_to_all(turned, "row", split_axis=1, concat_axis=1, tiled=True)
    spread = landed.reshape(groups, band_count, piece_len, piece_count, piece_len)
    placed = jnp.transpose(spread, (0, 3, 2, 1, 4))
    return placed.reshape(groups, rows_here, col_count)


def banded_body(packed, h_real, h_imag, h_cols):
    packed_here = packed.reshape(packed.shape[1], packed.shape[2])
    rows_here, col_count = packed_here.shape
    band_index = lax.axis_index("row")
    piece_index = lax.axis_index(("col", "sub"))
    piece_len = rows_here // lax.axis_size(("col", "sub"))
    flipped = mirror(packed_here[None])[0]
    row_ids = band_index * rows_here + jnp.arange(rows_here, dtype=jnp.int32)[:, None]
    col_local = jnp.arange(col_count, dtype=jnp.int32)[None, :]
    col_ids = col_local // piece_len * rows_here + piece_index * piece_len + col_local % piece_len
    upper_mask = row_ids <= col_ids
    real_part = jnp.where(upper_mask, packed_here, flipped)
    imag_part = jnp.where(
        row_ids > col_ids,
        packed_here,
        jnp.where(row_ids < col_ids, -flipped, jnp.zeros_like(flipped)),
    )
    current = jnp.stack([real_part, imag_part])
    summed = current.astype(jnp.float32)
    combined = jnp.stack([jnp.stack([h_imag, h_real], 2), jnp.stack([-h_real, h_imag], 2)])
    local_blocks = h_real.shape[0]
    block_len = h_real.shape[2]
    block_total = lax.axis_size("row") * local_blocks
    block_ids = band_index * local_blocks + jnp.arange(local_blocks, dtype=jnp.int32)[:, None]
    offsets = (h_cols - block_ids + 2) % block_total - 2
    starts = (
        (jnp.arange(local_blocks, dtype=jnp.int32)[:, None] + offsets + 2) * block_len
    ).reshape(-1)
    for term_index in range(1, TERMS + 1):
        padded = extended(current, (("row", 1),), 2 * block_len)
        sliced = jnp.stack(
            [
                lax.dynamic_slice_in_dim(padded, starts[k], block_len, 1)
                for k in range(starts.shape[0])
            ]
        )
        gathered = sliced.reshape(local_blocks, 4, 2, block_len, col_count)
        product = jnp.einsum(
            "obsgij,bsgjc->obic", combined, gathered, preferred_element_type=jnp.float32
        )
        generator = product.reshape(2, rows_here, col_count).astype(jnp.bfloat16)
        mirror_part = mirror(generator).astype(jnp.float32)
        own_part = generator.astype(jnp.float32)
        update = (
            step_size
            / term_index
            * jnp.stack([own_part[0] + mirror_part[0], own_part[1] - mirror_part[1]])
        )
        summed = summed + update
        current = update.astype(jnp.bfloat16)
    result = jnp.where(upper_mask, summed[0], summed[1])
    return result[None]


VMEM_BYTES = 56 * 2**20
NEAR_VMEM = 8 * 2**20
POWERS_VMEM = 20 * 2**20
MAIN_VMEM = 22 * 2**20
OWN_VMEM = 14 * 2**20
F32 = jnp.float32
BF16 = jnp.bfloat16


def exchange(block, axes, offset):
    count = lax.axis_size(axes)
    return lax.ppermute(block, axes, [(i, i ^ offset) for i in range(count)])


def block_product(dims, facts, h_refs, at, take):
    bands, rows, cols, piece, local, count, block, per = dims
    starts = []
    for side in (0, 1):
        for a in range(per):
            s = lax.bitwise_xor(facts[3], side) * per + a
            column = facts[4 + at * count + s]
            slot = lax.bitwise_xor(column // local, facts[0])
            starts.append(pl.multiple_of((slot * local + column % local) * block, block))
    right = jnp.concatenate([take(pl.ds(start, block)) for start in starts], axis=0)
    return jnp.dot(
        jnp.concatenate([ref[at] for ref in h_refs], axis=1), right, preferred_element_type=F32
    )


def apply_a(dims, facts, h_refs, at, take, width):
    block = dims[6]
    got = block_product(dims, facts, h_refs, at, take)
    real = got[:block, :width] + got[block:, width:]
    imag = got[:block, width:] - got[block:, :width]
    return 0.5 * jnp.concatenate([real, imag], axis=1)


def place_side(dims, facts, side, mine_ref, first_ref, part_ref, h_ref):
    bands, rows, cols, piece, local, count, block, per = dims
    core = lax.bitwise_xor(facts[3], side)
    wide = per * block
    for b in range(local):
        h_ref[b] = mine_ref[b, :, pl.ds(pl.multiple_of(core * wide, wide), wide)]
    for n in range(part_ref.shape[0] + 1):
        flat = (lax.bitwise_xor(facts[2], n) * 2 + core) * per
        below = pl.ds(pl.multiple_of((1 - flat // (local * count)) * block, block), block)
        b = flat // count % local
        for k in range(1, bands):
            for at in range(per):
                span = slice(at * block, (at + 1) * block)
                got = first_ref[k - 1, span, :] if n == 0 else part_ref[n - 1, k - 1, span, :]
                h_ref[k * local + b, below, span] = got


def near_kernel(dims, facts, mine_ref, first_ref, near_ref, h_ref, sel_ref):
    bands, rows, cols, piece, local, count, block, per = dims
    place_side(dims, facts, 0, mine_ref, first_ref, near_ref, h_ref)
    row_iota = lax.broadcasted_iota(jnp.int32, (rows, cols), 0)
    col_iota = lax.broadcasted_iota(jnp.int32, (rows, cols), 1)
    for k in range(bands):
        hit = (col_iota // piece == k) & (row_iota == facts[1] * piece + col_iota % piece)
        sel_ref[k * rows : (k + 1) * rows, :] = jnp.where(hit, 1.0, 0.0).astype(BF16)


def powers_kernel(dims, facts, mine_ref, first_ref, far_ref, near_h, sel, far_h, c_ref, c1_ref, c2_ref, csum):
    bands, rows, cols, piece, local, count, block, per = dims
    place_side(dims, facts, 1, mine_ref, first_ref, far_ref, far_h)
    h_refs = (near_h, far_h)

    def put_d(span, m, value):
        low = value.astype(BF16)
        c_ref[span, m * cols : (m + 1) * cols] = low[:, :cols]
        c_ref[span, (m + 3) * cols : (m + 4) * cols] = low[:, cols:]

    for at in range(bands * local):
        span = slice(at * block, (at + 1) * block)
        got = block_product(dims, facts, h_refs, at, lambda where: sel[where, :])
        c1 = 0.5 * jnp.concatenate([got[:block], -got[block:]], axis=1)
        c1_ref[span, :] = c1.astype(BF16)
        csum[span, :] = c1
        put_d(span, 2, 0.5 * c1)
    for at in range(bands * local):
        span = slice(at * block, (at + 1) * block)
        c2 = apply_a(dims, facts, h_refs, at, lambda where: c1_ref[where, :], cols)
        c2_ref[span, :] = c2.astype(BF16)
        both = csum[span, :] + 0.5 * c2
        csum[span, :] = both
        put_d(span, 1, both)
    for at in range(bands * local):
        span = slice(at * block, (at + 1) * block)
        c3 = apply_a(dims, facts, h_refs, at, lambda where: c2_ref[where, :], cols)
        put_d(span, 0, csum[span, :] + c3 * (1.0 / 6.0))


def swap_groups(value, r, piece):
    size = value.shape[1]
    groups = size // piece
    bit = 1
    while bit < groups:
        moved = jnp.concatenate(
            [value[:, (g ^ bit) * piece : (g ^ bit) * piece + piece] for g in range(groups)], axis=1
        )
        value = jnp.where(lax.bitwise_and(r, bit) != 0, moved, value)
        bit *= 2
    return value


def products(dims, facts, wanted, c_ref, n_ref, v1_ref, v2_ref, left, slab, outs):
    bands, rows, cols, piece, local, count, block, per = dims
    r, q = facts[0], facts[1]
    nt = (((1,), (1,)), ((), ()))
    size = len(wanted) * piece
    spans = [
        [pl.ds(pl.multiple_of(k * rows + p * piece, piece), piece) for p in wanted] for k in range(bands)
    ]
    i_own = lax.broadcasted_iota(jnp.int32, (piece, rows), 1)
    j_own = lax.broadcasted_iota(jnp.int32, (piece, rows), 0)
    upper = jnp.concatenate([i_own <= p * piece + j_own for p in wanted], axis=0)
    mine = lax.broadcasted_iota(jnp.int32, (size, rows), 1) // piece == q

    def against(which, slots):
        right = jnp.concatenate(
            [
                jnp.concatenate([ref[span, :] for ref in (c_ref, n_ref, v1_ref, v2_ref)], axis=1)
                for k in slots
                for span in spans[k]
            ],
            axis=0,
        )
        return lax.dot_general(right, left[which], nt, preferred_element_type=F32)

    for k in range(0, bands, 2):
        if k == 0:
            next_side = (lax.bitwise_xor(r, 1) < r).astype(jnp.int32)
            got = [jnp.where(upper, against(0, (0,)), against(1, (0,))), against(next_side, (1,))]
        else:
            side = against((lax.bitwise_xor(r, k) < r).astype(jnp.int32), (k, k + 1))
            got = [side[:size], side[size:]]
        for n in (0, 1):
            thin = jnp.concatenate([slab[span, :] for span in spans[k + n]], axis=0)
            real = jnp.concatenate([thin[:, :piece]] * (rows // piece), axis=1)
            imag = jnp.concatenate([-thin[:, piece:]] * (rows // piece), axis=1)
            above = upper if k + n == 0 else lax.bitwise_xor(r, k + n) > r
            outs[k + n] = got[n] + jnp.where(mine, jnp.where(above, real, imag), 0.0)

    def target(n):
        return jnp.concatenate(
            [outs[lax.bitwise_xor(r, b), n * piece : (n + 1) * piece, :] for b in range(bands)], axis=0
        ).T

    return target


def main_kernel(dims, facts, *refs):
    bands, rows, cols, piece, local, count, block, per = dims
    f_refs = refs[:bands]
    near_h, far_h, c_ref, keep_ref, send_ref, n_ref, v1_ref, v2_ref, left, slab, tops, outs = refs[bands:]
    h_refs = (near_h, far_h)
    r, q = facts[0], facts[1]
    row_iota = lax.broadcasted_iota(jnp.int32, (rows, cols), 0)
    col_iota = lax.broadcasted_iota(jnp.int32, (rows, cols), 1)
    col_abs = lax.bitwise_xor(col_iota // piece, r) * rows + q * piece + col_iota % piece
    for k in range(bands):
        here = swap_groups(f_refs[-k % bands][...].astype(F32), r, piece)
        row_abs = lax.bitwise_xor(r, k) * rows + row_iota
        real = jnp.where(row_abs < col_abs, here, jnp.where(row_abs == col_abs, 0.5 * here, 0.0))
        imag = jnp.where(row_abs > col_abs, here, 0.0)
        n_ref[k * rows : (k + 1) * rows, :] = jnp.concatenate([real, imag], axis=1).astype(BF16)

    def thin(value):
        return jnp.concatenate([value[:, :piece], value[:, cols : cols + piece]], axis=1)

    for at in range(bands * local):
        span = slice(at * block, (at + 1) * block)
        v1 = apply_a(dims, facts, h_refs, at, lambda where: n_ref[where, :], cols)
        v1_ref[span, :] = v1.astype(BF16)
        slab[span, :] = thin(v1)
        if at < local:
            tops[span, :] = v1
    for at in range(bands * local):
        span = slice(at * block, (at + 1) * block)
        v2 = apply_a(dims, facts, h_refs, at, lambda where: v1_ref[where, :], cols)
        v2_ref[span, :] = v2.astype(BF16)
        slab[span, :] += 0.5 * thin(v2)
        if at < local:
            tops[span, :] += 0.5 * v2
    for at in range(bands * local):
        span = slice(at * block, (at + 1) * block)
        v3 = apply_a(
            dims,
            facts,
            h_refs,
            at,
            lambda where: jnp.concatenate([v2_ref[where, 0:piece], v2_ref[where, cols : cols + piece]], axis=1),
            piece,
        )
        slab[span, :] += v3 * (1.0 / 6.0)
    own = slice(0, rows)
    three = 3 * cols
    for m, t_ref in enumerate((n_ref, v1_ref, v2_ref)):
        tr, ti = t_ref[own, :cols], t_ref[own, cols:]
        cr = c_ref[own, m * cols : (m + 1) * cols]
        ci = c_ref[own, three + m * cols : three + (m + 1) * cols]
        for which, (first, second, third, fourth) in enumerate(((tr, ti, cr, ci), (ti, -tr, ci, -cr))):
            left[which, :, m * cols : (m + 1) * cols] = first
            left[which, :, three + m * cols : three + (m + 1) * cols] = second
            left[which, :, 2 * three + 2 * m * cols : 2 * three + (2 * m + 1) * cols] = third
            left[which, :, 2 * three + (2 * m + 1) * cols : 2 * three + (2 * m + 2) * cols] = fourth
    far = lax.bitwise_xor(q, 2)
    wanted = (lax.bitwise_xor(far, 1), lax.bitwise_xor(q, 1), far)
    target = products(dims, facts, wanted, c_ref, n_ref, v1_ref, v2_ref, left, slab, outs)
    send_ref[0] = target(0).astype(BF16)
    send_ref[1] = target(1).astype(BF16)
    keep_ref[...] = target(2)


def own_kernel(dims, facts, near_h, far_h, c_ref, n_ref, v1_ref, v2_ref, left, slab, tops, own_ref, outs):
    bands, rows, cols, piece, local, count, block, per = dims
    r, q = facts[0], facts[1]
    target = products(dims, facts, (q,), c_ref, n_ref, v1_ref, v2_ref, left, slab, outs)
    col_iota = lax.broadcasted_iota(jnp.int32, (rows, cols), 1)
    col_abs = col_iota // piece * rows + q * piece + col_iota % piece
    row_abs = r * rows + lax.broadcasted_iota(jnp.int32, (rows, cols), 0)
    v3 = jnp.concatenate(
        [apply_a(dims, facts, (near_h, far_h), at, lambda where: v2_ref[where, :], cols) for at in range(local)],
        axis=0,
    )
    direct = tops[...] + v3 * (1.0 / 6.0)
    real = swap_groups(direct[:, :cols], r, piece)
    imag = swap_groups(direct[:, cols:], r, piece)
    own_ref[...] = target(0) + jnp.where(row_abs <= col_abs, real, imag)


def gathered_body(packed, h_real, h_imag, h_cols):
    here = packed.reshape(packed.shape[1], packed.shape[2])
    rows, cols = here.shape
    bands = lax.axis_size("row")
    piece = rows // lax.axis_size(("col", "sub"))
    local, count, block = h_real.shape[0], h_real.shape[1], h_real.shape[2]
    order = bands * rows
    r = lax.axis_index("row")
    q = lax.axis_index(("col", "sub"))
    me_plane = lax.axis_index(("runs", "col"))
    me_core = lax.axis_index("sub")
    shares = lax.axis_size(("runs", "col", "sub"))
    per = 2 * local * count // shares
    dims = (bands, rows, cols, piece, local, count, block, per)

    smem = pl.BlockSpec(memory_space=pltpu.SMEM)
    vmem = pl.BlockSpec(memory_space=pltpu.VMEM)
    flat_real, flat_imag = [h.reshape(local * count, block, block) for h in (h_real, h_imag)]

    def pick(first, second, at):
        return jnp.where(
            lax.axis_index("runs") == 0,
            lax.dynamic_slice_in_dim(first, at * per, per, 0),
            lax.dynamic_slice_in_dim(second, at * per, per, 0),
        ).reshape(per * block, block)

    size = per * block
    col_rows = jnp.pad(h_cols.astype(BF16), ((0, 16 - local), (0, block - count)))
    message = jnp.concatenate([pick(flat_real, flat_imag, q), col_rows], axis=0)
    diagonal = pick(flat_imag, flat_real, lax.bitwise_xor(q, 2))
    mine = jnp.concatenate(
        [h.transpose(0, 2, 1, 3).reshape(local, block, count * block) for h in (h_imag, h_real)], axis=1
    )
    arrived = [exchange(message, "row", k) for k in range(1, bands)]
    all_cols = [a[size : size + local, :count].astype(jnp.int32).reshape(-1) for a in [message] + arrived]
    facts = jnp.concatenate([jnp.stack([r, q, me_plane, me_core]).astype(jnp.int32)] + all_cols)
    theirs = lax.optimization_barrier(jnp.stack([a[:size] for a in arrived]))
    across_plane = jnp.concatenate([exchange(diagonal, "row", 1)[None], exchange(theirs[1:], ("runs", "col"), 3)], axis=0)
    near = jnp.stack([exchange(theirs, ("runs", "col"), k) for k in (1, 2)] + [across_plane])
    rest = [exchange(here, "row", k) for k in range(bands - 1, 0, -1)]
    first = exchange(theirs, "sub", 1)
    far = exchange(near, "sub", 1)

    step = 2 * order * 2 * count * block * 2 * cols
    half_shape = jax.ShapeDtypeStruct((bands * local, 2 * block, per * block), BF16)
    near_h, sel = pl.pallas_call(
        functools.partial(near_kernel, dims),
        out_shape=(half_shape, jax.ShapeDtypeStruct((order, cols), BF16)),
        in_specs=[smem] + [vmem] * 3,
        out_specs=(vmem, vmem),
        compiler_params=pltpu.CompilerParams(vmem_limit_bytes=NEAR_VMEM),
        cost_estimate=pl.CostEstimate(flops=0, bytes_accessed=2**20, transcendentals=0),
        name="near",
    )(facts, mine, theirs, near)
    far_h, c_side = pl.pallas_call(
        functools.partial(powers_kernel, dims),
        out_shape=(half_shape, jax.ShapeDtypeStruct((order, 6 * cols), BF16)),
        in_specs=[smem] + [vmem] * 5,
        out_specs=(vmem, vmem),
        scratch_shapes=[
            pltpu.VMEM((order, 2 * cols), BF16),
            pltpu.VMEM((order, 2 * cols), BF16),
            pltpu.VMEM((order, 2 * cols), F32),
        ],
        compiler_params=pltpu.CompilerParams(vmem_limit_bytes=POWERS_VMEM),
        cost_estimate=pl.CostEstimate(flops=5 * step // 2, bytes_accessed=2**20, transcendentals=0),
        name="powers",
    )(facts, mine, first, far, near_h, sel)
    block_shape = jax.ShapeDtypeStruct((rows, cols), F32)
    v_shape = jax.ShapeDtypeStruct((order, 2 * cols), BF16)
    keep, send, *state = pl.pallas_call(
        functools.partial(main_kernel, dims),
        out_shape=(
            block_shape,
            jax.ShapeDtypeStruct((2, rows, cols), BF16),
            v_shape,
            v_shape,
            v_shape,
            jax.ShapeDtypeStruct((2, rows, 12 * cols), BF16),
            jax.ShapeDtypeStruct((order, 2 * piece), F32),
            jax.ShapeDtypeStruct((rows, 2 * cols), F32),
        ),
        in_specs=[smem] + [vmem] * (bands + 3),
        out_specs=(vmem,) * 8,
        scratch_shapes=[pltpu.VMEM((bands, 3 * piece, rows), F32)],
        compiler_params=pltpu.CompilerParams(vmem_limit_bytes=MAIN_VMEM),
        cost_estimate=pl.CostEstimate(flops=4 * step, bytes_accessed=2**20, transcendentals=0),
        name="main",
    )(facts, here, *rest, near_h, far_h, c_side)
    swapped = exchange(send, "sub", 1)
    across = exchange((keep + swapped[0].astype(F32)).astype(BF16), "col", 1)
    own = pl.pallas_call(
        functools.partial(own_kernel, dims),
        out_shape=block_shape,
        in_specs=[smem] + [vmem] * 9,
        out_specs=vmem,
        scratch_shapes=[pltpu.VMEM((bands, piece, rows), F32)],
        compiler_params=pltpu.CompilerParams(vmem_limit_bytes=OWN_VMEM),
        cost_estimate=pl.CostEstimate(flops=step, bytes_accessed=2**20, transcendentals=0),
        name="own",
    )(facts, near_h, far_h, c_side, *state)
    total = here.astype(F32) + own + swapped[1].astype(F32) + across.astype(F32)
    return total[None]


def can_gather(mesh, local_packed, local_h):
    bands = mesh.shape["row"]
    rows, cols = local_packed[1], local_packed[2]
    local, count, block = local_h[0], local_h[1], local_h[2]
    shares = mesh.shape["runs"] * mesh.shape["col"] * mesh.shape["sub"]
    return (
        bands & (bands - 1) == 0
        and bands > 2
        and mesh.shape["runs"] == mesh.shape["col"] == mesh.shape["sub"] == 2
        and rows == cols == local * block
        and (2 * local * count) % shares == 0
        and local <= 16
        and count * shares == 4 * local * count
        and count <= block
        and 80 * bands * rows * bands * rows // 2 <= VMEM_BYTES
    )


def body(mesh, packed, h_real, h_imag, h_cols):
    if can_gather(mesh, packed.shape, h_real.shape):
        return gathered_body(packed, h_real, h_imag, h_cols)
    return banded_body(packed, h_real, h_imag, h_cols)


def solution(mesh):
    in_specs = (
        P(("col", "sub"), ("runs", "row"), None),
        P("row", None, None, None),
        P("row", None, None, None),
        P("row", None),
    )
    out_specs = P(("col", "sub"), ("runs", "row"), None)
    return jax.shard_map(
        functools.partial(body, mesh), mesh=mesh, in_specs=in_specs, out_specs=out_specs, check_vma=False
    )
```
